512 devices in a mesh: dp: 64 (over x, z, core), section: 8 (over y).
Axes of the slice: x: 4, y: 8, z: 8, core: 2. Of those that a mesh axis runs over, the one named last changes fastest.
Arguments:
- layer_input: bfloat16 [8, 64, 128, 4096], P('section', 'dp'), may hold values from -6 to 6
- keys: bfloat16 [8, 64, 128, 512], P('section', 'dp'), may hold values from -6 to 6
- values: bfloat16 [8, 64, 128, 512], P('section', 'dp'), may hold values from -6 to 6
- top_grad: bfloat16 [64, 128, 4096], P('dp'), may hold values from -6 to 6
- gains: float32 [8, 4096], P('section'), may hold values from 0.25 to 1.75
- biases: float32 [8, 4096], P('section'), may hold values from -4 to 4
- lengths: int32 [64], P('dp'), may hold values from 1 to 128, 5120 in all
Outputs:
- grad_in: bfloat16 [8, 64, 128, 4096], P('section', 'dp')
- key_grad: float32 [8, 64, 128, 512], P('section', 'dp')
- value_grad: float32 [8, 64, 128, 512], P('section', 'dp')
- gain_grad: float32 [8, 4096], P('section', 'dp')
- bias_grad: float32 [8, 4096], P('section', 'dp')
The draws below stay inside these ranges and needn't reach their ends.
Inputs may be any that keep to these rules, and one draw needn't show every extreme that they name: `lengths`: valid tokens of each request; some request has exactly 128.
All inputs are finite; a program needn't handle non-finite values. No bound on the sum of `lengths` on one device may be relied on, other than what follows from the above.
Results may differ from the reference program's by a relative error of at most 0.012.
Values may be sent and summed in bfloat16 or wider, within the bound.
A program may use at most 128 MiB of HBM per device.

```python
import math
import jax
import jax.numpy as jnp
import numpy as np
from jax import lax

HEADS = 32
KVH = 4
HD = 128
SEQ = 128
C = 4096
GROUP = 8
REQUESTS = 64
SECTIONS = 8
N_SECTION = 8


def draw_keys(key, part):
    key = jax.random.fold_in(key, 3)
    base = jnp.clip(jax.random.normal(key, (SECTIONS, REQUESTS, SEQ, KVH * HD), jnp.float32), -6.0, 6.0)
    return base.astype(jnp.bfloat16)


def draw_biases(key, part):
    key = jax.random.fold_in(key, 5)
    return jnp.clip(0.5 * jax.random.normal(key, (SECTIONS, HEADS * HD), jnp.float32), -3.0, 3.0)


def level_of(own_key, dims, shards, low, top_value):
    loudness, own = 1.0, jax.random.fold_in(own_key, 6)
    for dim, shards_of in shards:
        draws = jnp.exp(jax.random.uniform(jax.random.fold_in(own, dim), (shards_of,), jnp.float32, low / len(shards), top_value / len(shards)))
        loudness = loudness * jnp.repeat(draws, dims[dim] // shards_of).reshape([-1 if axis == dim else 1 for axis in range(len(dims))])
    return loudness


def split_up(amount, total, reach, slope):
    portions = [(1 << 20) // math.isqrt(grade ** slope) + 1 for grade in range(2, amount + 1)]
    rest, counts = total - reach - (amount - 1), [1] * (amount - 1)
    while rest > 0:
        candidates = [i for i in range(amount - 1) if counts[i] < reach]
        whole, remaining = sum([portions[i] for i in candidates]), rest
        for i in candidates:
            addition = min(reach - counts[i], max(1, remaining * portions[i] // whole), rest)
            counts[i] = counts[i] + addition
            rest = rest - addition
    return np.array([reach] + counts)


def uneven(key, number_of, total, limit, slope):
    if number_of == 2:
        one = jax.random.randint(key, (), max(1, total - limit), min(limit, total - 1) + 1)
        return jnp.stack([one, total - one])
    sizes = jnp.asarray(split_up(number_of, total, limit, slope), jnp.int32)
    twos = (number_of - 1) // 2
    donor, taker = sizes[1:1 + 2 * twos:2], sizes[2:2 + 2 * twos:2]
    slack = jnp.minimum(donor - 1, limit - taker)
    passed = jax.random.randint(jax.random.fold_in(key, 1), (twos,), 0, 1 << 20) % (slack + 1)
    sizes = sizes.at[1:1 + 2 * twos:2].set(donor - passed).at[2:2 + 2 * twos:2].set(taker + passed)
    return sizes[jax.random.permutation(jax.random.fold_in(key, 2), number_of)]


def normal_values(rng, dims, deviation, bound, pieces=(), kind=jnp.bfloat16):
    loudness = level_of(rng, dims, pieces, -0.22, 0.18) if pieces else 1.0
    drawn = jax.random.normal(rng, dims, jnp.float32) * deviation * loudness
    return jnp.minimum(jnp.maximum(drawn, -bound), bound).astype(kind)


def setup_inputs(seed: int = 0) -> dict:
    key_of = jax.random.split(jax.random.key(seed), 8)
    layer_input = normal_values(key_of[0], (SECTIONS, REQUESTS, SEQ, C), 1.0, 6.0, ((0, 8), (1, 64)))
    keys = draw_keys(jax.random.fold_in(key_of[7], 71), 0)
    values = normal_values(key_of[2], (SECTIONS, REQUESTS, SEQ, KVH * HD), 1.0, 6.0, ((0, 8), (1, 64)))
    top_grad = normal_values(key_of[3], (REQUESTS, SEQ, C), 1.0, 6.0, ((0, 64),))
    gains = jnp.clip(1.0 + 0.15 * jax.random.normal(key_of[4], (SECTIONS, C), jnp.float32), 0.25, 1.75)
    biases = draw_biases(jax.random.fold_in(key_of[7], 71), 0)
    lengths = uneven(key_of[6], REQUESTS, REQUESTS * SEQ * 5 // 8, SEQ, 2).astype(jnp.int32)
    return {"layer_input": layer_input, "keys": keys, "values": values, "top_grad": top_grad, "gains": gains, "biases": biases, "lengths": lengths}


def mixed(form, left, right):
    return jnp.einsum(form, left.astype(jnp.float32), right.astype(jnp.float32), precision=lax.Precision.HIGHEST)

def block_grad(upstream, start, layer_rows, key_rows, value_rows, gain, bias, length):
    count = upstream.shape[0]
    seqlen = key_rows.shape[0]
    inputs = lax.dynamic_slice_in_dim(layer_rows, start, count, 0).astype(jnp.float32)
    inverse = lax.rsqrt(lax.optimization_barrier(jnp.mean(inputs * inputs, -1, keepdims=True)) + 1e-06)
    normed = inputs * inverse
    query = (normed * gain + bias).astype(jnp.bfloat16)
    query_heads = query.reshape(count, KVH, GROUP, HD)
    key_heads = key_rows.reshape(seqlen, KVH, HD)
    value_heads = value_rows.reshape(seqlen, KVH, HD)
    factor = HD ** (-0.5)
    scores = mixed('ikgd,jkd->kgij', query_heads, key_heads) * factor
    positions = start + jnp.arange(count, dtype=jnp.int32)
    columns = jnp.arange(seqlen, dtype=jnp.int32)
    allowed = (columns[None, :] <= positions[:, None]) & (columns[None, :] < length)
    scores = jnp.where(allowed, scores, -1e+30)
    peak = lax.optimization_barrier(jnp.max(scores, -1, keepdims=True))
    weights = jnp.exp(scores - peak)
    weights = weights / lax.optimization_barrier(jnp.sum(weights, -1, keepdims=True))
    live = positions < length
    weights = weights * live[:, None].astype(jnp.float32)
    grad_out = jnp.where(live[:, None], upstream, jnp.zeros_like(upstream))
    grad_heads = grad_out.reshape(count, KVH, GROUP, HD)
    grad_probs = mixed('ikgd,jkd->kgij', grad_heads, value_heads)
    centre = lax.optimization_barrier(jnp.sum(weights * grad_probs, -1, keepdims=True))
    grad_scores = (weights * (grad_probs - centre) * factor).astype(jnp.bfloat16)
    grad_query = mixed('kgij,jkd->ikgd', grad_scores, key_heads).reshape(count, -1)
    key_part = mixed('kgij,ikgd->jkd', grad_scores, query_heads).reshape(seqlen, -1)
    value_part = mixed('kgij,ikgd->jkd', weights.astype(jnp.bfloat16), grad_heads).reshape(seqlen, -1)
    bias_part = lax.optimization_barrier(jnp.sum(grad_query, 0))
    gain_part = lax.optimization_barrier(jnp.sum(grad_query * normed, 0))
    scaled = grad_query * gain
    grad_inputs = inverse * (scaled - normed * lax.optimization_barrier(jnp.mean(scaled * normed, -1, keepdims=True)))
    result = (upstream.astype(jnp.float32) + grad_inputs).astype(jnp.bfloat16)
    return (result, key_part, value_part, gain_part, bias_part)

def reference(layer_input, keys, values, top_grad, gains, biases, lengths):
    upstream = top_grad
    grad_list, key_list, value_list, gain_list, bias_list = ([], [], [], [], [])
    for layer in reversed(range(N_SECTION)):
        gain = gains[layer]
        bias = biases[layer]

        def single(items):
            return block_grad(items[3], 0, items[0], items[1], items[2], gain, bias, items[4])
        result, key_part, value_part, gain_part, bias_part = lax.map(single, (layer_input[layer], keys[layer], values[layer], upstream, lengths))
        grad_list.insert(0, result)
        key_list.insert(0, key_part)
        value_list.insert(0, value_part)
        gain_list.insert(0, lax.optimization_barrier(jnp.sum(gain_part, 0)))
        bias_list.insert(0, lax.optimization_barrier(jnp.sum(bias_part, 0)))
        upstream = result
    return (jnp.stack(grad_list), jnp.stack(key_list), jnp.stack(value_list), jnp.stack(gain_list), jnp.stack(bias_list))
```

```python
import functools

import jax
import jax.numpy as jnp
from jax import lax
from jax.experimental import pallas as pl
from jax.experimental.pallas import tpu as pltpu
from jax.sharding import PartitionSpec as P

MESH = pl.DeviceIdType.MESH
HD = 128
KVH = 4
SEQ = 128
WIDTH = 4096
ROWS = 4
SPANS = SEQ // ROWS
BLOCK = 16
BLOCKS = SEQ // BLOCK
PER_BLOCK = BLOCK // ROWS
HALF = 16
DP_X, DP_Z, DP_CORE = 4, 8, 2
FACTOR = HD ** (-0.5)
F32, BF16 = jnp.float32, jnp.bfloat16


def dot(a, b):
    return jnp.dot(a, b, preferred_element_type=F32)


def low_of(rows):
    return (lax.broadcasted_iota(jnp.int32, (rows, HD), 0) & 7) < 4


def pick(wide, low):
    return jnp.where(low, wide[:, :HD], wide[:, HD:])


def spread(narrow, low):
    zero = jnp.zeros_like(narrow)
    return jnp.concatenate([jnp.where(low, narrow, zero), jnp.where(low, zero, narrow)], axis=1)


def tiled(eight, times):
    return jnp.concatenate([eight] * times, axis=0)


def pack(eight_rows, low8):
    first, second = [], []
    for h in range(HALF):
        a = eight_rows[:, h * HD : (h + 1) * HD]
        b = eight_rows[:, (h + HALF) * HD : (h + HALF + 1) * HD]
        first.append(jnp.where(low8, a, pltpu.roll(b, 4, 0)))
        second.append(jnp.where(low8, pltpu.roll(a, 4, 0), b))
    return jnp.concatenate(first, axis=0), jnp.concatenate(second, axis=0)


def kernel(
    sections,
    x_hbm, k_hbm, v_hbm, top_hbm, gain_hbm, bias_hbm, length_ref,
    out_ref, key_out, value_out, gain_out, bias_out,
    x_v, top_v, k_v, v_v, gain_v, bias_v,
    keys, values, keys_t, values_t, gain_p, bias_p,
    arrived, sent, norm_p, inv_p, probs_p, mix_p, base_p,
    query_b, probs_b, grads_b, gain_acc, bias_acc,
    first_src, first_dst, second_src, second_dst,
    in_sem, x_sem, top_sem, send_sem, recv_sem, s1_send, s1_recv, s2_send, s2_recv,
):
    section = lax.axis_index("section")
    me = lax.axis_index("dp")
    px, pz, pc = me // 16, (me // 2) % 8, me % 2
    above, below = (section + 1) % sections, (section + sections - 1) % sections
    is_top = section == sections - 1

    def x_copy(b):
        rows = pl.ds(b * BLOCK, BLOCK)
        return pltpu.make_async_copy(x_hbm.at[rows], x_v.at[rows], x_sem.at[b])

    def top_copy(b):
        rows = pl.ds(b * BLOCK, BLOCK)
        return pltpu.make_async_copy(top_hbm.at[rows], top_v.at[rows], top_sem.at[b])

    small = [
        pltpu.make_async_copy(src, dst, in_sem.at[i])
        for i, (src, dst) in enumerate(
            [(k_hbm, k_v), (v_hbm, v_v), (gain_hbm, gain_v), (bias_hbm, bias_v)]
        )
    ]
    for copy in small:
        copy.start()
    for b in range(BLOCKS):
        x_copy(b).start()

    @pl.when(is_top)
    def _():
        for b in range(BLOCKS):
            top_copy(b).start()

    def first_peer(k):
        return {"dp": px * 16 + ((pz + k // 2) % 8) * 2 + (pc + k % 2) % 2}

    def second_peer(k):
        return {"dp": ((px + k) % 4) * 16 + pz * 2 + pc}

    barrier = pltpu.get_barrier_semaphore()
    peers = [{"section": above}, {"section": below}]
    peers += [first_peer(k) for k in range(1, 16)] + [second_peer(k) for k in range(1, 4)]
    for peer in peers:
        pl.semaphore_signal(barrier, inc=1, device_id=peer, device_id_type=MESH)

    low8, low64, low128 = low_of(8), low_of(64), low_of(128)
    for copy in small:
        copy.wait()
    for p in range(2):
        for src, dst, dst_t in ((k_v, keys, keys_t), (v_v, values, values_t)):
            for j in range(2):
                part = src[:, (p + 2 * j) * HD : (p + 2 * j + 1) * HD]
                dst[p, j * SEQ : (j + 1) * SEQ, :] = part
                dst_t[p, :, j * SEQ : (j + 1) * SEQ] = part.T
    for src, dst in ((gain_v, gain_p), (bias_v, bias_p)):
        for h in range(HALF):
            a = jnp.broadcast_to(src[:, h * HD : (h + 1) * HD], (8, HD))
            b = jnp.broadcast_to(src[:, (h + HALF) * HD : (h + HALF + 1) * HD], (8, HD))
            dst[h * 8 : (h + 1) * 8, :] = jnp.where(low8, a, b)
    gain_acc[...] = jnp.zeros_like(gain_acc)
    bias_acc[...] = jnp.zeros_like(bias_acc)
    length = length_ref[0]
    columns = lax.broadcasted_iota(jnp.int32, (8, HD), 1)
    offsets = lax.broadcasted_iota(jnp.int32, (8, HD), 0) & 3

    pl.semaphore_wait(barrier, len(peers))

    def forward(b):
        x_copy(b).wait()
        inputs = x_v[pl.ds(b * BLOCK, BLOCK), :].astype(F32)
        inverse = lax.rsqrt(jnp.mean(inputs * inputs, -1, keepdims=True) + 1e-06)
        normed = inputs * inverse
        inverse = jnp.broadcast_to(inverse, (BLOCK, HD))
        gains, biases = gain_p[...], bias_p[...]
        for half in range(2):
            rows = slice(half * 8, half * 8 + 8)
            pair = pack(normed[rows], low8)
            inv = inverse[rows]
            flipped = pltpu.roll(inv, 4, 0)
            pair_inv = (jnp.where(low8, inv, flipped), jnp.where(low8, flipped, inv))
            for j in range(2):
                span = b * PER_BLOCK + half * 2 + j
                norm = pair[j]
                norm_p[span] = norm
                inv_p[span] = pair_inv[j]
                gained = norm * gains
                query = (gained + biases).astype(BF16)
                gained = gained.astype(BF16)
                position = span * ROWS + offsets
                live = tiled(jnp.where(position < length, 1.0, 0.0).astype(F32), 8)
                allowed = tiled(
                    jnp.where((columns <= position) & (columns < length), 1.0, 0.0).astype(F32), 8
                )
                for p in range(2):
                    part = slice(64 * p, 64 * p + 64)
                    query_b[p, span] = query[part]
                    both = dot(jnp.concatenate([query[part], gained[part]], axis=0), keys_t[p])
                    both = pick(both, low128)
                    scores = jnp.where(allowed > 0.5, both[:64] * FACTOR, -1e30)
                    mix_p[span, part, :] = both[64:]
                    weights = jnp.exp(scores - jnp.max(scores, -1, keepdims=True))
                    weights = weights * (1.0 / jnp.sum(weights, -1, keepdims=True)) * live
                    probs_p[span, part, :] = weights * FACTOR
                    wide = spread(weights, low64)
                    high = wide.astype(BF16)
                    probs_b[p, span] = high
                    rest = (wide - high.astype(F32)).astype(BF16)
                    outs = dot(jnp.concatenate([high, rest], axis=0), values[p])
                    base_p[span, part, :] = outs[:64] + outs[64:]

    def take_top(b):
        top_copy(b).wait()
        rows = top_v[pl.ds(b * BLOCK, BLOCK), :].astype(F32)
        for half in range(2):
            pair = pack(rows[half * 8 : half * 8 + 8], low8)
            for j in range(2):
                arrived[b * PER_BLOCK + half * 2 + j] = pair[j].astype(BF16)

    def hop(i):
        return pltpu.make_async_remote_copy(
            src_ref=sent.at[i],
            dst_ref=arrived.at[i],
            send_sem=send_sem.at[i],
            recv_sem=recv_sem.at[i],
            device_id={"section": below},
            device_id_type=MESH,
        )

    def backward(i):
        @pl.when(jnp.logical_not(is_top))
        def _():
            hop(i).wait_recv()

        upstream = arrived[i]
        wide = upstream.astype(F32)
        centre = jnp.sum(wide * base_p[i], -1, keepdims=True)
        queries, kept, totals = [], [], jnp.zeros((8, HD), F32)
        for p in range(2):
            part = slice(64 * p, 64 * p + 64)
            grad_probs = pick(dot(upstream[part], values_t[p]), low64)
            grads = probs_p[i, part, :] * (grad_probs - centre[part])
            totals = totals + jnp.sum((grads * mix_p[i, part, :]).reshape(8, 8, HD), axis=0)
            grads_wide = spread(grads, low64).astype(BF16)
            kept.append(grads_wide)
            queries.append(dot(grads_wide, keys[p]))
        mean = jnp.sum(totals, -1, keepdims=True) * (1.0 / WIDTH)
        mean = jnp.broadcast_to(mean, (8, HD))
        mean = mean + pltpu.roll(mean, 4, 0)
        grad_query = jnp.concatenate(queries, axis=0)
        norm = norm_p[i]
        change = grad_query * gain_p[...] - norm * tiled(mean, HALF)
        sent[i] = (wide + tiled(inv_p[i], HALF) * change).astype(BF16)

        @pl.when(section > 0)
        def _():
            hop(i).start()

        for p in range(2):
            grads_b[p, i] = kept[p]
        gain_acc[...] += grad_query * norm
        bias_acc[...] += grad_query

    lead = jnp.where(is_top, 0, jnp.where(section == sections - 2, 2, BLOCKS - 1))

    def turn(t, carry):
        @pl.when(t < BLOCKS)
        def _():
            @pl.when(is_top)
            def _():
                take_top(t)

            forward(t)

        @pl.when(t >= lead)
        def _():
            def step(q, c):
                backward((t - lead) * PER_BLOCK + q)
                return c

            lax.fori_loop(0, PER_BLOCK, step, 0)

        return carry

    lax.fori_loop(0, BLOCKS + lead, turn, 0)

    for g, acc in enumerate((gain_acc, bias_acc)):
        terms = acc[...].reshape(HALF, 8, HD)
        halves = (jnp.sum(terms[:, :4], axis=1), jnp.sum(terms[:, 4:], axis=1))
        for x in range(DP_X):
            rows = halves[x // 2][(x % 2) * 8 : (x % 2) * 8 + 8]
            for z in range(DP_Z):
                first_src[z, 2 * x + g : 2 * x + g + 1, :] = rows[z : z + 1]

    def first_copy(k):
        return pltpu.make_async_remote_copy(
            src_ref=first_src.at[(pz + k // 2) % 8],
            dst_ref=first_dst.at[k],
            send_sem=s1_send.at[k],
            recv_sem=s1_recv.at[k],
            device_id=first_peer(k),
            device_id_type=MESH,
        )

    def second_copy(k):
        return pltpu.make_async_remote_copy(
            src_ref=second_src.at[(px + k) % 4],
            dst_ref=second_dst.at[k],
            send_sem=s2_send.at[k],
            recv_sem=s2_recv.at[k],
            device_id=second_peer(k),
            device_id_type=MESH,
        )

    for k in range(1, 16):
        first_copy(k).start()

    flat = SPANS * 64

    def contract(left, right):
        return lax.dot_general(left, right, (((0,), (0,)), ((), ())), preferred_element_type=F32)

    for p in range(2):
        got = arrived[:, 64 * p : 64 * p + 64, :].reshape(flat, HD)
        value_grad = contract(probs_b[p].reshape(flat, 2 * SEQ), got)
        for j in range(2):
            head = p + 2 * j
            value_out[:, head * HD : (head + 1) * HD] = value_grad[j * SEQ : (j + 1) * SEQ]

    total = first_src[pz]
    for k in range(1, 16):
        first_copy(k).wait_recv()
        total = total + first_dst[k]
    for x in range(DP_X):
        second_src[x] = total[2 * x : 2 * x + 2]
    for k in range(1, 4):
        second_copy(k).start()

    for p in range(2):
        key_grad = contract(grads_b[p].reshape(flat, 2 * SEQ), query_b[p].reshape(flat, HD))
        for j in range(2):
            head = p + 2 * j
            key_out[:, head * HD : (head + 1) * HD] = key_grad[j * SEQ : (j + 1) * SEQ]

    def unpack(b, carry):
        parts = [sent[b * PER_BLOCK + j].astype(F32) for j in range(PER_BLOCK)]
        for h in range(HALF):
            tiles = [part[h * 8 : h * 8 + 8] for part in parts]
            turned = [pltpu.roll(tile, 4, 0) for tile in tiles]
            lower = [jnp.where(low8, tiles[j], turned[j + 1]) for j in (0, 2)]
            upper = [jnp.where(low8, turned[j], tiles[j + 1]) for j in (0, 2)]
            for head, pieces in ((h, lower), (h + HALF, upper)):
                out_ref[pl.ds(b * BLOCK, BLOCK), head * HD : (head + 1) * HD] = jnp.concatenate(
                    pieces, axis=0
                ).astype(BF16)
        return carry

    lax.fori_loop(0, BLOCKS, unpack, 0)

    share = second_src[px]
    for k in range(1, 4):
        second_copy(k).wait_recv()
        share = share + second_dst[k]
    share = jnp.where(pc == 0, share, pltpu.roll(share, HD // 2, 1))
    gain_out[...] = share[0:1, : HD // 2]
    bias_out[...] = share[1:2, : HD // 2]

    def sent_all(i, carry):
        hop(i).wait_send()
        return carry

    @pl.when(section > 0)
    def _():
        lax.fori_loop(0, SPANS, sent_all, 0)

    for k in range(1, 16):
        first_copy(k).wait_send()
    for k in range(1, 4):
        second_copy(k).wait_send()


def local(sections, layer_input, keys, values, top_grad, gains, biases, lengths):
    anywhere = pl.BlockSpec(memory_space=pl.ANY)
    vmem = pl.BlockSpec(memory_space=pltpu.VMEM)
    kv = KVH * HD
    dma = pltpu.SemaphoreType.DMA
    span = (SPANS, 128, HD)
    outs = pl.pallas_call(
        functools.partial(kernel, sections),
        out_shape=(
            jax.ShapeDtypeStruct((SEQ, WIDTH), BF16),
            jax.ShapeDtypeStruct((SEQ, kv), F32),
            jax.ShapeDtypeStruct((SEQ, kv), F32),
            jax.ShapeDtypeStruct((1, HD // 2), F32),
            jax.ShapeDtypeStruct((1, HD // 2), F32),
        ),
        in_specs=[anywhere] * 6 + [pl.BlockSpec(memory_space=pltpu.SMEM)],
        out_specs=(vmem,) * 5,
        scratch_shapes=[
            pltpu.VMEM((SEQ, WIDTH), BF16),
            pltpu.VMEM((SEQ, WIDTH), BF16),
            pltpu.VMEM((SEQ, kv), BF16),
            pltpu.VMEM((SEQ, kv), BF16),
            pltpu.VMEM((1, WIDTH), F32),
            pltpu.VMEM((1, WIDTH), F32),
            pltpu.VMEM((2, 2 * SEQ, HD), BF16),
            pltpu.VMEM((2, 2 * SEQ, HD), BF16),
            pltpu.VMEM((2, HD, 2 * SEQ), BF16),
            pltpu.VMEM((2, HD, 2 * SEQ), BF16),
            pltpu.VMEM((128, HD), F32),
            pltpu.VMEM((128, HD), F32),
            pltpu.VMEM(span, BF16),
            pltpu.VMEM(span, BF16),
            pltpu.VMEM(span, F32),
            pltpu.VMEM((SPANS, 8, HD), F32),
            pltpu.VMEM(span, F32),
            pltpu.VMEM(span, F32),
            pltpu.VMEM(span, F32),
            pltpu.VMEM((2, SPANS, 64, HD), BF16),
            pltpu.VMEM((2, SPANS, 64, 2 * SEQ), BF16),
            pltpu.VMEM((2, SPANS, 64, 2 * SEQ), BF16),
            pltpu.VMEM((128, HD), F32),
            pltpu.VMEM((128, HD), F32),
            pltpu.VMEM((DP_Z, 8, HD), F32),
            pltpu.VMEM((16, 8, HD), F32),
            pltpu.VMEM((DP_X, 2, HD), F32),
            pltpu.VMEM((DP_X, 2, HD), F32),
            dma((4,)),
            dma((BLOCKS,)),
            dma((BLOCKS,)),
            dma((SPANS,)),
            dma((SPANS,)),
            dma((16,)),
            dma((16,)),
            dma((4,)),
            dma((4,)),
        ],
        compiler_params=pltpu.CompilerParams(
            collective_id=0, has_side_effects=True, vmem_limit_bytes=48 << 20
        ),
    )(layer_input[0, 0], keys[0, 0], values[0, 0], top_grad[0], gains, biases, lengths)
    grad_in, key_grad, value_grad, gain_grad, bias_grad = outs
    return grad_in[None, None], key_grad[None, None], value_grad[None, None], gain_grad, bias_grad


def solution(mesh):
    return jax.shard_map(
        functools.partial(local, mesh.shape["section"]),
        mesh=mesh,
        in_specs=(
            P("section", "dp", None, None),
            P("section", "dp", None, None),
            P("section", "dp", None, None),
            P("dp", None, None),
            P("section", None),
            P("section", None),
            P("dp"),
        ),
        out_specs=(
            P("section", "dp", None, None),
            P("section", "dp", None, None),
            P("section", "dp", None, None),
            P("section", "dp"),
            P("section", "dp"),
        ),
        check_vma=False,
    )
```

```python
import functools

import jax
import jax.numpy as jnp
from jax import lax
from jax.experimental import pallas as pl
from jax.experimental.pallas import tpu as pltpu
from jax.sharding import PartitionSpec as P

MESH = pl.DeviceIdType.MESH
HD = 128
KVH = 4
SEQ = 128
WIDTH = 4096
ROWS = 4
SPANS = SEQ // ROWS
BLOCK = 16
BLOCKS = SEQ // BLOCK
PER_BLOCK = BLOCK // ROWS
HALF = 16
DP_X, DP_Z, DP_CORE = 4, 8, 2
FACTOR = HD ** (-0.5)
F32, BF16 = jnp.float32, jnp.bfloat16


def dot(a, b):
    return jnp.dot(a, b, preferred_element_type=F32)


def low_of(rows):
    return (lax.broadcasted_iota(jnp.int32, (rows, HD), 0) & 7) < 4


def pick(wide, low):
    return jnp.where(low, wide[:, :HD], wide[:, HD:])


def spread(narrow, low):
    zero = jnp.zeros_like(narrow)
    return jnp.concatenate([jnp.where(low, narrow, zero), jnp.where(low, zero, narrow)], axis=1)


def tiled(eight, times):
    return jnp.concatenate([eight] * times, axis=0)


def pack(eight_rows, low8):
    first, second = [], []
    for h in range(HALF):
        a = eight_rows[:, h * HD : (h + 1) * HD]
        b = eight_rows[:, (h + HALF) * HD : (h + HALF + 1) * HD]
        first.append(jnp.where(low8, a, pltpu.roll(b, 4, 0)))
        second.append(jnp.where(low8, pltpu.roll(a, 4, 0), b))
    return jnp.concatenate(first, axis=0), jnp.concatenate(second, axis=0)


def kernel(
    sections,
    x_hbm, k_hbm, v_hbm, top_hbm, gain_hbm, bias_hbm, length_ref,
    out_ref, key_out, value_out, gain_out, bias_out,
    x_v, top_v, k_v, v_v, gain_v, bias_v,
    keys, values, keys_t, values_t, gain_p, bias_p,
    arrived, sent, norm_p, inv_p, probs_p, mix_p, base_p,
    query_b, probs_b, grads_b, gain_acc, bias_acc,
    first_src, first_dst, second_src, second_dst,
    in_sem, x_sem, top_sem, send_sem, recv_sem, s1_send, s1_recv, s2_send, s2_recv,
):
    section = lax.axis_index("section")
    me = lax.axis_index("dp")
    px, pz, pc = me // 16, (me // 2) % 8, me % 2
    above, below = (section + 1) % sections, (section + sections - 1) % sections
    is_top = section == sections - 1
    held_back = is_top & (pc == 1)

    def x_copy(b):
        rows = pl.ds(b * BLOCK, BLOCK)
        return pltpu.make_async_copy(x_hbm.at[rows], x_v.at[rows], x_sem.at[b])

    def top_copy(b):
        rows = pl.ds(b * BLOCK, BLOCK)
        return pltpu.make_async_copy(top_hbm.at[rows], top_v.at[rows], top_sem.at[b])

    small = [
        pltpu.make_async_copy(src, dst, in_sem.at[i])
        for i, (src, dst) in enumerate(
            [(k_hbm, k_v), (v_hbm, v_v), (gain_hbm, gain_v), (bias_hbm, bias_v)]
        )
    ]
    for copy in small:
        copy.start()
    for b in range(BLOCKS):
        x_copy(b).start()

    @pl.when(is_top)
    def _():
        for b in range(BLOCKS):
            top_copy(b).start()

    def first_peer(k):
        return {"dp": px * 16 + ((pz + k // 2) % 8) * 2 + (pc + k % 2) % 2}

    def second_peer(k):
        return {"dp": ((px + k // 2) % 4) * 16 + pz * 2 + (pc + k % 2) % 2}

    barrier = pltpu.get_barrier_semaphore()
    peers = [{"section": above}, {"section": below}]
    peers += [first_peer(k) for k in range(1, 16)] + [second_peer(k) for k in range(2, 8)]
    for peer in peers:
        pl.semaphore_signal(barrier, inc=1, device_id=peer, device_id_type=MESH)

    low8, low64, low128 = low_of(8), low_of(64), low_of(128)
    for copy in small:
        copy.wait()
    for p in range(2):
        for src, dst, dst_t in ((k_v, keys, keys_t), (v_v, values, values_t)):
            for j in range(2):
                part = src[:, (p + 2 * j) * HD : (p + 2 * j + 1) * HD]
                dst[p, j * SEQ : (j + 1) * SEQ, :] = part
                dst_t[p, :, j * SEQ : (j + 1) * SEQ] = part.T
    for src, dst in ((gain_v, gain_p), (bias_v, bias_p)):
        for h in range(HALF):
            a = jnp.broadcast_to(src[:, h * HD : (h + 1) * HD], (8, HD))
            b = jnp.broadcast_to(src[:, (h + HALF) * HD : (h + HALF + 1) * HD], (8, HD))
            dst[h * 8 : (h + 1) * 8, :] = jnp.where(low8, a, b)
    gain_acc[...] = jnp.zeros_like(gain_acc)
    bias_acc[...] = jnp.zeros_like(bias_acc)
    length = length_ref[0]
    columns = lax.broadcasted_iota(jnp.int32, (8, HD), 1)
    offsets = lax.broadcasted_iota(jnp.int32, (8, HD), 0) & 3

    def forward(b):
        x_copy(b).wait()
        inputs = x_v[pl.ds(b * BLOCK, BLOCK), :].astype(F32)
        inverse = lax.rsqrt(jnp.mean(inputs * inputs, -1, keepdims=True) + 1e-06)
        normed = inputs * inverse
        inverse = jnp.broadcast_to(inverse, (BLOCK, HD))
        gains, biases = gain_p[...], bias_p[...]
        for half in range(2):
            rows = slice(half * 8, half * 8 + 8)
            pair = pack(normed[rows], low8)
            inv = inverse[rows]
            flipped = pltpu.roll(inv, 4, 0)
            pair_inv = (jnp.where(low8, inv, flipped), jnp.where(low8, flipped, inv))
            for j in range(2):
                span = b * PER_BLOCK + half * 2 + j
                norm = pair[j]
                norm_p[span] = norm
                inv_p[span] = pair_inv[j]
                gained = norm * gains
                query = (gained + biases).astype(BF16)
                gained = gained.astype(BF16)
                position = span * ROWS + offsets
                live = tiled(jnp.where(position < length, 1.0, 0.0).astype(F32), 8)
                allowed = tiled(
                    jnp.where((columns <= position) & (columns < length), 1.0, 0.0).astype(F32), 8
                )
                for p in range(2):
                    part = slice(64 * p, 64 * p + 64)
                    query_b[p, span] = query[part]
                    both = dot(jnp.concatenate([query[part], gained[part]], axis=0), keys_t[p])
                    both = pick(both, low128)
                    scores = jnp.where(allowed > 0.5, both[:64] * FACTOR, -1e30)
                    mix_p[span, part, :] = both[64:]
                    weights = jnp.exp(scores - jnp.max(scores, -1, keepdims=True))
                    weights = weights * (1.0 / jnp.sum(weights, -1, keepdims=True)) * live
                    probs_p[span, part, :] = weights * FACTOR
                    wide = spread(weights, low64)
                    high = wide.astype(BF16)
                    probs_b[p, span] = high
                    rest = (wide - high.astype(F32)).astype(BF16)
                    outs = dot(jnp.concatenate([high, rest], axis=0), values[p])
                    base_p[span, part, :] = outs[:64] + outs[64:]

    def take_top(b):
        top_copy(b).wait()
        rows = top_v[pl.ds(b * BLOCK, BLOCK), :].astype(F32)
        for half in range(2):
            pair = pack(rows[half * 8 : half * 8 + 8], low8)
            for j in range(2):
                arrived[b * PER_BLOCK + half * 2 + j] = pair[j].astype(BF16)

    def hop(i):
        return pltpu.make_async_remote_copy(
            src_ref=sent.at[i],
            dst_ref=arrived.at[i],
            send_sem=send_sem.at[i],
            recv_sem=recv_sem.at[i],
            device_id={"section": below},
            device_id_type=MESH,
        )

    def backward(i):
        @pl.when(jnp.logical_not(is_top))
        def _():
            hop(i).wait_recv()

        upstream = arrived[i]
        wide = upstream.astype(F32)
        centre = jnp.sum(wide * base_p[i], -1, keepdims=True)
        queries, kept, totals = [], [], jnp.zeros((8, HD), F32)
        for p in range(2):
            part = slice(64 * p, 64 * p + 64)
            grad_probs = pick(dot(upstream[part], values_t[p]), low64)
            grads = probs_p[i, part, :] * (grad_probs - centre[part])
            totals = totals + jnp.sum((grads * mix_p[i, part, :]).reshape(8, 8, HD), axis=0)
            grads_wide = spread(grads, low64).astype(BF16)
            kept.append(grads_wide)
            queries.append(dot(grads_wide, keys[p]))
        mean = jnp.sum(totals, -1, keepdims=True) * (1.0 / WIDTH)
        mean = jnp.broadcast_to(mean, (8, HD))
        mean = mean + pltpu.roll(mean, 4, 0)
        grad_query = jnp.concatenate(queries, axis=0)
        norm = norm_p[i]
        change = grad_query * gain_p[...] - norm * tiled(mean, HALF)
        sent[i] = (wide + tiled(inv_p[i], HALF) * change).astype(BF16)

        @pl.when((section > 0) & jnp.logical_not(held_back))
        def _():
            hop(i).start()

        @pl.when(held_back & (i % 2 == 1))
        def _():
            hop(i // 2).start()

        for p in range(2):
            grads_b[p, i] = kept[p]
        gain_acc[...] += grad_query * norm
        bias_acc[...] += grad_query

    behind = sections - 1 - section
    lead = jnp.where(behind == 0, 0, jnp.where(behind == 1, 3, jnp.where(behind == 2, 6, BLOCKS - 1)))

    def prepare(b):
        @pl.when(is_top)
        def _():
            take_top(b)

        forward(b)

    prepare(0)
    pl.semaphore_wait(barrier, len(peers))

    def turn(t, carry):
        @pl.when(t >= lead)
        def _():
            def step(q, c):
                backward((t - lead) * PER_BLOCK + q)
                return c

            lax.fori_loop(0, PER_BLOCK, step, 0)

        @pl.when(t + 1 < BLOCKS)
        def _():
            prepare(t + 1)

        return carry

    lax.fori_loop(0, BLOCKS + lead, turn, 0)

    @pl.when(held_back)
    def _():
        def late(i, carry):
            hop(i).start()
            return carry

        lax.fori_loop(SPANS // 2, SPANS, late, 0)

    for g, acc in enumerate((gain_acc, bias_acc)):
        terms = acc[...].reshape(HALF, 8, HD)
        halves = (jnp.sum(terms[:, :4], axis=1), jnp.sum(terms[:, 4:], axis=1))
        for x in range(DP_X):
            rows = halves[x // 2][(x % 2) * 8 : (x % 2) * 8 + 8]
            for z in range(DP_Z):
                first_src[g, z, x : x + 1, :] = rows[z : z + 1]

    def first_copy(k):
        return pltpu.make_async_remote_copy(
            src_ref=first_src.at[(pc + k % 2) % 2, (pz + k // 2) % 8],
            dst_ref=first_dst.at[k],
            send_sem=s1_send.at[k],
            recv_sem=s1_recv.at[k],
            device_id=first_peer(k),
            device_id_type=MESH,
        )

    def second_copy(k):
        return pltpu.make_async_remote_copy(
            src_ref=second_src.at[(px + k // 2) % 4],
            dst_ref=second_dst.at[k],
            send_sem=s2_send.at[k],
            recv_sem=s2_recv.at[k],
            device_id=second_peer(k),
            device_id_type=MESH,
        )

    for k in range(1, 16):
        first_copy(k).start()

    flat = SPANS * 64

    def contract(left, right):
        return lax.dot_general(left, right, (((0,), (0,)), ((), ())), preferred_element_type=F32)

    for p in range(2):
        got = arrived[:, 64 * p : 64 * p + 64, :].reshape(flat, HD)
        value_grad = contract(probs_b[p].reshape(flat, 2 * SEQ), got)
        for j in range(2):
            head = p + 2 * j
            value_out[:, head * HD : (head + 1) * HD] = value_grad[j * SEQ : (j + 1) * SEQ]

    total = first_src[pc, pz]
    for k in range(1, 16):
        first_copy(k).wait_recv()
        total = total + first_dst[k]
    for x in range(DP_X):
        second_src[x] = total[x : x + 1]
    for k in range(1, 8):
        second_copy(k).start()

    for p in range(2):
        key_grad = contract(grads_b[p].reshape(flat, 2 * SEQ), query_b[p].reshape(flat, HD))
        for j in range(2):
            head = p + 2 * j
            key_out[:, head * HD : (head + 1) * HD] = key_grad[j * SEQ : (j + 1) * SEQ]

    def unpack(b, carry):
        parts = [sent[b * PER_BLOCK + j].astype(F32) for j in range(PER_BLOCK)]
        for h in range(HALF):
            tiles = [part[h * 8 : h * 8 + 8] for part in parts]
            turned = [pltpu.roll(tile, 4, 0) for tile in tiles]
            lower = [jnp.where(low8, tiles[j], turned[j + 1]) for j in (0, 2)]
            upper = [jnp.where(low8, turned[j], tiles[j + 1]) for j in (0, 2)]
            for head, pieces in ((h, lower), (h + HALF, upper)):
                out_ref[pl.ds(b * BLOCK, BLOCK), head * HD : (head + 1) * HD] = jnp.concatenate(
                    pieces, axis=0
                ).astype(BF16)
        return carry

    lax.fori_loop(0, BLOCKS, unpack, 0)

    shares = [second_src[px], jnp.zeros((1, HD), F32)]
    for k in range(1, 8):
        second_copy(k).wait_recv()
        shares[k % 2] = shares[k % 2] + second_dst[k]
    gain = jnp.where(pc == 0, shares[0], pltpu.roll(shares[1], HD // 2, 1))
    bias = jnp.where(pc == 0, shares[1], pltpu.roll(shares[0], HD // 2, 1))
    gain_out[...] = gain[:, : HD // 2]
    bias_out[...] = bias[:, : HD // 2]

    def sent_all(i, carry):
        hop(i).wait_send()
        return carry

    @pl.when(section > 0)
    def _():
        lax.fori_loop(0, SPANS, sent_all, 0)

    for k in range(1, 16):
        first_copy(k).wait_send()
    for k in range(1, 8):
        second_copy(k).wait_send()


def write(*refs):
    count = len(refs) // 2
    copies = [
        pltpu.make_async_copy(refs[i], refs[count + i], refs[-1].at[i]) for i in range(count)
    ]
    for copy in copies:
        copy.start()
    for copy in copies:
        copy.wait()


def local(sections, layer_input, keys, values, top_grad, gains, biases, lengths):
    anywhere = pl.BlockSpec(memory_space=pltpu.HBM)
    vmem = pl.BlockSpec(memory_space=pltpu.VMEM)
    kv = KVH * HD
    dma = pltpu.SemaphoreType.DMA
    span = (SPANS, 128, HD)
    outs = pl.pallas_call(
        functools.partial(kernel, sections),
        out_shape=(
            jax.ShapeDtypeStruct((SEQ, WIDTH), BF16),
            jax.ShapeDtypeStruct((SEQ, kv), F32),
            jax.ShapeDtypeStruct((SEQ, kv), F32),
            jax.ShapeDtypeStruct((1, HD // 2), F32),
            jax.ShapeDtypeStruct((1, HD // 2), F32),
        ),
        in_specs=[anywhere] * 6 + [pl.BlockSpec(memory_space=pltpu.SMEM)],
        out_specs=(vmem,) * 5,
        scratch_shapes=[
            pltpu.VMEM((SEQ, WIDTH), BF16),
            pltpu.VMEM((SEQ, WIDTH), BF16),
            pltpu.VMEM((SEQ, kv), BF16),
            pltpu.VMEM((SEQ, kv), BF16),
            pltpu.VMEM((1, WIDTH), F32),
            pltpu.VMEM((1, WIDTH), F32),
            pltpu.VMEM((2, 2 * SEQ, HD), BF16),
            pltpu.VMEM((2, 2 * SEQ, HD), BF16),
            pltpu.VMEM((2, HD, 2 * SEQ), BF16),
            pltpu.VMEM((2, HD, 2 * SEQ), BF16),
            pltpu.VMEM((128, HD), F32),
            pltpu.VMEM((128, HD), F32),
            pltpu.VMEM(span, BF16),
            pltpu.VMEM(span, BF16),
            pltpu.VMEM(span, F32),
            pltpu.VMEM((SPANS, 8, HD), F32),
            pltpu.VMEM(span, F32),
            pltpu.VMEM(span, F32),
            pltpu.VMEM(span, F32),
            pltpu.VMEM((2, SPANS, 64, HD), BF16),
            pltpu.VMEM((2, SPANS, 64, 2 * SEQ), BF16),
            pltpu.VMEM((2, SPANS, 64, 2 * SEQ), BF16),
            pltpu.VMEM((128, HD), F32),
            pltpu.VMEM((128, HD), F32),
            pltpu.VMEM((DP_CORE, DP_Z, DP_X, HD), F32),
            pltpu.VMEM((DP_Z * DP_CORE, DP_X, HD), F32),
            pltpu.VMEM((DP_X, 1, HD), F32),
            pltpu.VMEM((DP_X * DP_CORE, 1, HD), F32),
            dma((4,)),
            dma((BLOCKS,)),
            dma((BLOCKS,)),
            dma((SPANS,)),
            dma((SPANS,)),
            dma((16,)),
            dma((16,)),
            dma((8,)),
            dma((8,)),
        ],
        compiler_params=pltpu.CompilerParams(
            collective_id=0, has_side_effects=True, vmem_limit_bytes=40 << 20
        ),
    )(*[pltpu.with_memory_space_constraint(a, pltpu.HBM) for a in (layer_input[0, 0], keys[0, 0], values[0, 0], top_grad[0], gains, biases)], lengths)
    grad_in, key_grad, value_grad, gain_grad, bias_grad = pl.pallas_call(
        write,
        out_shape=tuple(jax.ShapeDtypeStruct(out.shape, out.dtype) for out in outs),
        in_specs=[vmem] * len(outs),
        out_specs=(anywhere,) * len(outs),
        scratch_shapes=[dma((len(outs),))],
        compiler_params=pltpu.CompilerParams(vmem_limit_bytes=4 << 20),
    )(*outs)
    return grad_in[None, None], key_grad[None, None], value_grad[None, None], gain_grad, bias_grad


def solution(mesh):
    return jax.shard_map(
        functools.partial(local, mesh.shape["section"]),
        mesh=mesh,
        in_specs=(
            P("section", "dp", None, None),
            P("section", "dp", None, None),
            P("section", "dp", None, None),
            P("dp", None, None),
            P("section", None),
            P("section", None),
            P("dp"),
        ),
        out_specs=(
            P("section", "dp", None, None),
            P("section", "dp", None, None),
            P("section", "dp", None, None),
            P("section", "dp"),
            P("section", "dp"),
        ),
        check_vma=False,
    )
```

```python
import functools

import jax
import jax.numpy as jnp
from jax import lax
from jax.experimental import pallas as pl
from jax.experimental.pallas import tpu as pltpu
from jax.sharding import PartitionSpec as P

MESH = pl.DeviceIdType.MESH
HD = 128
KVH = 4
SEQ = 128
WIDTH = 4096
ROWS = 4
SPANS = SEQ // ROWS
BLOCK = 16
BLOCKS = SEQ // BLOCK
PER_BLOCK = BLOCK // ROWS
HALF = 16
DP_X, DP_Z, DP_CORE = 4, 8, 2
FACTOR = HD ** (-0.5)
F32, BF16 = jnp.float32, jnp.bfloat16
OFFSETS = sorted(
    ((x, z, core) for x in range(DP_X) for z in range(DP_Z) for core in range(DP_CORE)),
    key=lambda at: (-min(at[0], DP_X - at[0]) - min(at[1], DP_Z - at[1]), at),
)
OFFSETS.remove((0, 0, 0))
PARTNERS = len(OFFSETS)


def dot(a, b):
    return jnp.dot(a, b, preferred_element_type=F32)


def low_of(rows):
    return (lax.broadcasted_iota(jnp.int32, (rows, HD), 0) & 7) < 4


def pick(wide, low):
    return jnp.where(low, wide[:, :HD], wide[:, HD:])


def spread(narrow, low):
    zero = jnp.zeros_like(narrow)
    return jnp.concatenate([jnp.where(low, narrow, zero), jnp.where(low, zero, narrow)], axis=1)


def tiled(eight, times):
    return jnp.concatenate([eight] * times, axis=0)


def pack(eight_rows, low8):
    first, second = [], []
    for h in range(HALF):
        a = eight_rows[:, h * HD : (h + 1) * HD]
        b = eight_rows[:, (h + HALF) * HD : (h + HALF + 1) * HD]
        first.append(jnp.where(low8, a, pltpu.roll(b, 4, 0)))
        second.append(jnp.where(low8, pltpu.roll(a, 4, 0), b))
    return jnp.concatenate(first, axis=0), jnp.concatenate(second, axis=0)


def kernel(
    sections,
    x_hbm, k_hbm, v_hbm, top_hbm, gain_hbm, bias_hbm, length_ref,
    out_ref, key_out, value_out, gain_out, bias_out,
    x_v, top_v, k_v, v_v, gain_v, bias_v,
    keys, values, keys_t, values_t, gain_p, bias_p,
    arrived, sent, norm_p, inv_p, probs_p, mix_p, base_p,
    query_b, probs_b, grads_b, gain_acc, bias_acc,
    share_src, share_dst,
    in_sem, x_sem, top_sem, send_sem, recv_sem, share_sem,
):
    section = lax.axis_index("section")
    me = lax.axis_index("dp")
    px, pz, pc = me // 16, (me // 2) % 8, me % 2
    above, below = (section + 1) % sections, (section + sections - 1) % sections
    is_top = section == sections - 1
    held_back = is_top & (pc == 1)

    def x_copy(b):
        rows = pl.ds(b * BLOCK, BLOCK)
        return pltpu.make_async_copy(x_hbm.at[rows], x_v.at[rows], x_sem.at[b])

    def top_copy(b):
        rows = pl.ds(b * BLOCK, BLOCK)
        return pltpu.make_async_copy(top_hbm.at[rows], top_v.at[rows], top_sem.at[b])

    small = [
        pltpu.make_async_copy(src, dst, in_sem.at[i])
        for i, (src, dst) in enumerate(
            [(k_hbm, k_v), (v_hbm, v_v), (gain_hbm, gain_v), (bias_hbm, bias_v)]
        )
    ]
    for copy in small:
        copy.start()
    for b in range(BLOCKS):
        x_copy(b).start()

    @pl.when(is_top)
    def _():
        for b in range(BLOCKS):
            top_copy(b).start()

    def partner(k):
        x, z, core = OFFSETS[k]
        return ((px + x) % DP_X) * 16 + ((pz + z) % DP_Z) * 2 + (pc + core) % DP_CORE

    barrier = pltpu.get_barrier_semaphore()
    peers = [{"section": above}, {"section": below}]
    peers += [{"dp": partner(k)} for k in range(PARTNERS)]
    for peer in peers:
        pl.semaphore_signal(barrier, inc=1, device_id=peer, device_id_type=MESH)

    low8, low64, low128 = low_of(8), low_of(64), low_of(128)
    for copy in small:
        copy.wait()
    for p in range(2):
        for src, dst, dst_t in ((k_v, keys, keys_t), (v_v, values, values_t)):
            for j in range(2):
                part = src[:, (p + 2 * j) * HD : (p + 2 * j + 1) * HD]
                dst[p, j * SEQ : (j + 1) * SEQ, :] = part
                dst_t[p, :, j * SEQ : (j + 1) * SEQ] = part.T
    for src, dst in ((gain_v, gain_p), (bias_v, bias_p)):
        for h in range(HALF):
            a = jnp.broadcast_to(src[:, h * HD : (h + 1) * HD], (8, HD))
            b = jnp.broadcast_to(src[:, (h + HALF) * HD : (h + HALF + 1) * HD], (8, HD))
            dst[h * 8 : (h + 1) * 8, :] = jnp.where(low8, a, b)
    gain_acc[...] = jnp.zeros_like(gain_acc)
    bias_acc[...] = jnp.zeros_like(bias_acc)
    length = length_ref[0]
    columns = lax.broadcasted_iota(jnp.int32, (8, HD), 1)
    offsets = lax.broadcasted_iota(jnp.int32, (8, HD), 0) & 3

    def forward(b):
        x_copy(b).wait()
        inputs = x_v[pl.ds(b * BLOCK, BLOCK), :].astype(F32)
        inverse = lax.rsqrt(jnp.mean(inputs * inputs, -1, keepdims=True) + 1e-06)
        normed = inputs * inverse
        inverse = jnp.broadcast_to(inverse, (BLOCK, HD))
        gains, biases = gain_p[...], bias_p[...]
        for half in range(2):
            rows = slice(half * 8, half * 8 + 8)
            pair = pack(normed[rows], low8)
            inv = inverse[rows]
            flipped = pltpu.roll(inv, 4, 0)
            pair_inv = (jnp.where(low8, inv, flipped), jnp.where(low8, flipped, inv))
            for j in range(2):
                span = b * PER_BLOCK + half * 2 + j
                norm = pair[j]
                norm_p[span] = norm
                inv_p[span] = pair_inv[j]
                gained = norm * gains
                query = (gained + biases).astype(BF16)
                gained = gained.astype(BF16)
                position = span * ROWS + offsets
                live = tiled(jnp.where(position < length, 1.0, 0.0).astype(F32), 8)
                allowed = tiled(
                    jnp.where((columns <= position) & (columns < length), 1.0, 0.0).astype(F32), 8
                )
                for p in range(2):
                    part = slice(64 * p, 64 * p + 64)
                    query_b[p, span] = query[part]
                    both = dot(jnp.concatenate([query[part], gained[part]], axis=0), keys_t[p])
                    both = pick(both, low128)
                    scores = jnp.where(allowed > 0.5, both[:64] * FACTOR, -1e30)
                    mix_p[span, part, :] = both[64:]
                    weights = jnp.exp(scores - jnp.max(scores, -1, keepdims=True))
                    weights = weights * (1.0 / jnp.sum(weights, -1, keepdims=True)) * live
                    probs_p[span, part, :] = weights * FACTOR
                    wide = spread(weights, low64)
                    high = wide.astype(BF16)
                    probs_b[p, span] = high
                    rest = (wide - high.astype(F32)).astype(BF16)
                    outs = dot(jnp.concatenate([high, rest], axis=0), values[p])
                    base_p[span, part, :] = outs[:64] + outs[64:]

    def take_top(b):
        top_copy(b).wait()
        rows = top_v[pl.ds(b * BLOCK, BLOCK), :].astype(F32)
        for half in range(2):
            pair = pack(rows[half * 8 : half * 8 + 8], low8)
            for j in range(2):
                arrived[b * PER_BLOCK + half * 2 + j] = pair[j].astype(BF16)

    def hop(i):
        return pltpu.make_async_remote_copy(
            src_ref=sent.at[i],
            dst_ref=arrived.at[i],
            send_sem=send_sem.at[i],
            recv_sem=recv_sem.at[i],
            device_id={"section": below},
            device_id_type=MESH,
        )

    def backward(i):
        @pl.when(jnp.logical_not(is_top))
        def _():
            hop(i).wait_recv()

        upstream = arrived[i]
        wide = upstream.astype(F32)
        centre = jnp.sum(wide * base_p[i], -1, keepdims=True)
        queries, kept, totals = [], [], jnp.zeros((8, HD), F32)
        for p in range(2):
            part = slice(64 * p, 64 * p + 64)
            grad_probs = pick(dot(upstream[part], values_t[p]), low64)
            grads = probs_p[i, part, :] * (grad_probs - centre[part])
            totals = totals + jnp.sum((grads * mix_p[i, part, :]).reshape(8, 8, HD), axis=0)
            grads_wide = spread(grads, low64).astype(BF16)
            kept.append(grads_wide)
            queries.append(dot(grads_wide, keys[p]))
        mean = jnp.sum(totals, -1, keepdims=True) * (1.0 / WIDTH)
        mean = jnp.broadcast_to(mean, (8, HD))
        mean = mean + pltpu.roll(mean, 4, 0)
        grad_query = jnp.concatenate(queries, axis=0)
        norm = norm_p[i]
        change = grad_query * gain_p[...] - norm * tiled(mean, HALF)
        sent[i] = (wide + tiled(inv_p[i], HALF) * change).astype(BF16)

        @pl.when((section > 0) & jnp.logical_not(held_back))
        def _():
            hop(i).start()

        @pl.when(held_back & ((2 * i) % 3 > 0))
        def _():
            hop((2 * i + 2) // 3 - 1).start()

        for p in range(2):
            grads_b[p, i] = kept[p]
        gain_acc[...] += grad_query * norm
        bias_acc[...] += grad_query

    behind = sections - 1 - section
    lead = jnp.where(behind == 0, 0, jnp.where(behind == 1, 3, jnp.where(behind == 2, 6, BLOCKS - 1)))

    def prepare(b):
        @pl.when(is_top)
        def _():
            take_top(b)

        forward(b)

    prepare(0)
    pl.semaphore_wait(barrier, len(peers))

    def turn(t, carry):
        @pl.when(t >= lead)
        def _():
            def step(q, c):
                backward((t - lead) * PER_BLOCK + q)
                return c

            lax.fori_loop(0, PER_BLOCK, step, 0)

        @pl.when(t + 1 < BLOCKS)
        def _():
            prepare(t + 1)

        return carry

    lax.fori_loop(0, BLOCKS + lead, turn, 0)

    @pl.when(held_back)
    def _():
        def late(i, carry):
            hop(i).start()
            return carry

        lax.fori_loop(SPANS * 2 // 3, SPANS, late, 0)

    left = lax.broadcasted_iota(jnp.int32, (HALF, HD), 1) < HD // 2
    gain_terms, bias_terms = (acc[...].reshape(HALF, 8, HD) for acc in (gain_acc, bias_acc))
    for j in range(2):
        gain = jnp.sum(gain_terms[:, 4 * j : 4 * j + 4], axis=1)
        bias = jnp.sum(bias_terms[:, 4 * j : 4 * j + 4], axis=1)
        rows = (
            jnp.where(left, gain, pltpu.roll(bias, HD // 2, 1)),
            jnp.where(left, pltpu.roll(gain, HD // 2, 1), bias),
        )
        for h in range(HALF):
            for core in range(DP_CORE):
                share_src[2 * (HALF * j + h) + core] = rows[core][h : h + 1]

    def share_copy(k):
        return pltpu.make_async_remote_copy(
            src_ref=share_src.at[partner(k)],
            dst_ref=share_dst.at[k],
            send_sem=share_sem.at[0],
            recv_sem=share_sem.at[1],
            device_id={"dp": partner(k)},
            device_id_type=MESH,
        )

    for k in range(PARTNERS):
        share_copy(k).start()

    flat = SPANS * 64

    def contract(left, right):
        return lax.dot_general(left, right, (((0,), (0,)), ((), ())), preferred_element_type=F32)

    for p in range(2):
        got = arrived[:, 64 * p : 64 * p + 64, :].reshape(flat, HD)
        value_grad = contract(probs_b[p].reshape(flat, 2 * SEQ), got)
        for j in range(2):
            head = p + 2 * j
            value_out[:, head * HD : (head + 1) * HD] = value_grad[j * SEQ : (j + 1) * SEQ]

    for p in range(2):
        key_grad = contract(grads_b[p].reshape(flat, 2 * SEQ), query_b[p].reshape(flat, HD))
        for j in range(2):
            head = p + 2 * j
            key_out[:, head * HD : (head + 1) * HD] = key_grad[j * SEQ : (j + 1) * SEQ]

    def unpack(b, carry):
        parts = [sent[b * PER_BLOCK + j].astype(F32) for j in range(PER_BLOCK)]
        for h in range(HALF):
            tiles = [part[h * 8 : h * 8 + 8] for part in parts]
            turned = [pltpu.roll(tile, 4, 0) for tile in tiles]
            lower = [jnp.where(low8, tiles[j], turned[j + 1]) for j in (0, 2)]
            upper = [jnp.where(low8, turned[j], tiles[j + 1]) for j in (0, 2)]
            for head, pieces in ((h, lower), (h + HALF, upper)):
                out_ref[pl.ds(b * BLOCK, BLOCK), head * HD : (head + 1) * HD] = jnp.concatenate(
                    pieces, axis=0
                ).astype(BF16)
        return carry

    lax.fori_loop(0, BLOCKS, unpack, 0)

    pltpu.make_async_copy(share_dst, share_dst, share_sem.at[1]).wait()
    share = share_src[me] + jnp.sum(share_dst[...], axis=0)
    gain_out[...] = share[:, : HD // 2]
    bias_out[...] = pltpu.roll(share, HD // 2, 1)[:, : HD // 2]

    def sent_all(i, carry):
        hop(i).wait_send()
        return carry

    @pl.when(section > 0)
    def _():
        lax.fori_loop(0, SPANS, sent_all, 0)

    pltpu.make_async_copy(share_dst, share_dst, share_sem.at[0]).wait()


def write(*refs):
    count = len(refs) // 2
    copies = [
        pltpu.make_async_copy(refs[i], refs[count + i], refs[-1].at[i]) for i in range(count)
    ]
    for copy in copies:
        copy.start()
    for copy in copies:
        copy.wait()


def local(sections, layer_input, keys, values, top_grad, gains, biases, lengths):
    anywhere = pl.BlockSpec(memory_space=pltpu.HBM)
    vmem = pl.BlockSpec(memory_space=pltpu.VMEM)
    kv = KVH * HD
    dma = pltpu.SemaphoreType.DMA
    span = (SPANS, 128, HD)
    outs = pl.pallas_call(
        functools.partial(kernel, sections),
        out_shape=(
            jax.ShapeDtypeStruct((SEQ, WIDTH), BF16),
            jax.ShapeDtypeStruct((SEQ, kv), F32),
            jax.ShapeDtypeStruct((SEQ, kv), F32),
            jax.ShapeDtypeStruct((1, HD // 2), F32),
            jax.ShapeDtypeStruct((1, HD // 2), F32),
        ),
        in_specs=[anywhere] * 6 + [pl.BlockSpec(memory_space=pltpu.SMEM)],
        out_specs=(vmem,) * 5,
        scratch_shapes=[
            pltpu.VMEM((SEQ, WIDTH), BF16),
            pltpu.VMEM((SEQ, WIDTH), BF16),
            pltpu.VMEM((SEQ, kv), BF16),
            pltpu.VMEM((SEQ, kv), BF16),
            pltpu.VMEM((1, WIDTH), F32),
            pltpu.VMEM((1, WIDTH), F32),
            pltpu.VMEM((2, 2 * SEQ, HD), BF16),
            pltpu.VMEM((2, 2 * SEQ, HD), BF16),
            pltpu.VMEM((2, HD, 2 * SEQ), BF16),
            pltpu.VMEM((2, HD, 2 * SEQ), BF16),
            pltpu.VMEM((128, HD), F32),
            pltpu.VMEM((128, HD), F32),
            pltpu.VMEM(span, BF16),
            pltpu.VMEM(span, BF16),
            pltpu.VMEM(span, F32),
            pltpu.VMEM((SPANS, 8, HD), F32),
            pltpu.VMEM(span, F32),
            pltpu.VMEM(span, F32),
            pltpu.VMEM(span, F32),
            pltpu.VMEM((2, SPANS, 64, HD), BF16),
            pltpu.VMEM((2, SPANS, 64, 2 * SEQ), BF16),
            pltpu.VMEM((2, SPANS, 64, 2 * SEQ), BF16),
            pltpu.VMEM((128, HD), F32),
            pltpu.VMEM((128, HD), F32),
            pltpu.VMEM((PARTNERS + 1, 1, HD), F32),
            pltpu.VMEM((PARTNERS, 1, HD), F32),
            dma((4,)),
            dma((BLOCKS,)),
            dma((BLOCKS,)),
            dma((SPANS,)),
            dma((SPANS,)),
            dma((2,)),
        ],
        compiler_params=pltpu.CompilerParams(
            collective_id=0, has_side_effects=True, vmem_limit_bytes=40 << 20
        ),
    )(*[pltpu.with_memory_space_constraint(a, pltpu.HBM) for a in (layer_input[0, 0], keys[0, 0], values[0, 0], top_grad[0], gains, biases)], lengths)
    grad_in, key_grad, value_grad, gain_grad, bias_grad = pl.pallas_call(
        write,
        out_shape=tuple(jax.ShapeDtypeStruct(out.shape, out.dtype) for out in outs),
        in_specs=[vmem] * len(outs),
        out_specs=(anywhere,) * len(outs),
        scratch_shapes=[dma((len(outs),))],
        compiler_params=pltpu.CompilerParams(vmem_limit_bytes=4 << 20),
    )(*outs)
    return grad_in[None, None], key_grad[None, None], value_grad[None, None], gain_grad, bias_grad


def solution(mesh):
    return jax.shard_map(
        functools.partial(local, mesh.shape["section"]),
        mesh=mesh,
        in_specs=(
            P("section", "dp", None, None),
            P("section", "dp", None, None),
            P("section", "dp", None, None),
            P("dp", None, None),
            P("section", None),
            P("section", None),
            P("dp"),
        ),
        out_specs=(
            P("section", "dp", None, None),
            P("section", "dp", None, None),
            P("section", "dp", None, None),
            P("section", "dp"),
            P("section", "dp"),
        ),
        check_vma=False,
    )
```

```python
import functools

import jax
import jax.numpy as jnp
from jax import lax
from jax.experimental import pallas as pl
from jax.experimental.pallas import tpu as pltpu
from jax.sharding import PartitionSpec as P

MESH = pl.DeviceIdType.MESH
HD = 128
KVH = 4
SEQ = 128
WIDTH = 4096
ROWS = 4
SPANS = SEQ // ROWS
BLOCK = 16
BLOCKS = SEQ // BLOCK
PER_BLOCK = BLOCK // ROWS
HALF = 16
DP_X, DP_Z, DP_CORE = 4, 8, 2
FACTOR = HD ** (-0.5)
F32, BF16 = jnp.float32, jnp.bfloat16
OFFSETS = sorted(
    ((x, z, core) for x in range(DP_X) for z in range(DP_Z) for core in range(DP_CORE)),
    key=lambda at: (-min(at[0], DP_X - at[0]) - min(at[1], DP_Z - at[1]), at),
)
OFFSETS.remove((0, 0, 0))
PARTNERS = len(OFFSETS)
NEXT = ((0, 1, 0), (0, 7, 0), (1, 0, 0), (3, 0, 0), (0, 0, 1))
ROUNDS = (
    ((0, 1, 0), (0, 7, 0), (1, 0, 0), (3, 0, 0)),
    ((0, 2, 0), (0, 6, 0)),
    ((1, 0, 0), (3, 0, 0), (2, 0, 0)),
    ((0, 0, 1),),
)


def dot(a, b):
    return jnp.dot(a, b, preferred_element_type=F32)


def low_of(rows):
    return (lax.broadcasted_iota(jnp.int32, (rows, HD), 0) & 7) < 4


def pick(wide, low):
    return jnp.where(low, wide[:, :HD], wide[:, HD:])


def spread(narrow, low):
    zero = jnp.zeros_like(narrow)
    return jnp.concatenate([jnp.where(low, narrow, zero), jnp.where(low, zero, narrow)], axis=1)


def tiled(eight, times):
    return jnp.concatenate([eight] * times, axis=0)


def pack(eight_rows, low8):
    first, second = [], []
    for h in range(HALF):
        a = eight_rows[:, h * HD : (h + 1) * HD]
        b = eight_rows[:, (h + HALF) * HD : (h + HALF + 1) * HD]
        first.append(jnp.where(low8, a, pltpu.roll(b, 4, 0)))
        second.append(jnp.where(low8, pltpu.roll(a, 4, 0), b))
    return jnp.concatenate(first, axis=0), jnp.concatenate(second, axis=0)


def kernel(
    sections,
    x_hbm, k_hbm, v_hbm, top_hbm, gain_hbm, bias_hbm, length_ref,
    out_ref, key_out, value_out, gain_out, bias_out,
    x_v, top_v, k_v, v_v, gain_v, bias_v,
    keys, values, keys_t, values_t, gain_p, bias_p,
    arrived, sent, norm_p, inv_p, probs_p, mix_p, base_p,
    query_b, probs_b, grads_b, gain_acc, bias_acc,
    share_src, share_dst,
    in_sem, x_sem, top_sem, send_sem, recv_sem, share_sem, round_sem,
):
    section = lax.axis_index("section")
    me = lax.axis_index("dp")
    px, pz, pc = me // 16, (me // 2) % 8, me % 2
    above, below = (section + 1) % sections, (section + sections - 1) % sections
    is_top = section == sections - 1
    held_back = is_top & (pc == 1)

    def x_copy(b):
        rows = pl.ds(b * BLOCK, BLOCK)
        return pltpu.make_async_copy(x_hbm.at[rows], x_v.at[rows], x_sem.at[b])

    def top_copy(b):
        rows = pl.ds(b * BLOCK, BLOCK)
        return pltpu.make_async_copy(top_hbm.at[rows], top_v.at[rows], top_sem.at[b])

    small = [
        pltpu.make_async_copy(src, dst, in_sem.at[i])
        for i, (src, dst) in enumerate(
            [(k_hbm, k_v), (v_hbm, v_v), (gain_hbm, gain_v), (bias_hbm, bias_v)]
        )
    ]
    for copy in small:
        copy.start()
    for b in range(BLOCKS):
        x_copy(b).start()

    @pl.when(is_top)
    def _():
        for b in range(BLOCKS):
            top_copy(b).start()

    def partner(k):
        x, z, core = OFFSETS[k]
        return ((px + x) % DP_X) * 16 + ((pz + z) % DP_Z) * 2 + (pc + core) % DP_CORE

    def place(x, z, core):
        return {"dp": ((px + x) % DP_X) * 16 + ((pz + z) % DP_Z) * 2 + (pc + core) % DP_CORE}

    def tell(r):
        for x, z, core in ROUNDS[r]:
            pl.semaphore_signal(
                round_sem.at[r], inc=1, device_id=place(x, z, core), device_id_type=MESH
            )

    def hear(r):
        pl.semaphore_wait(round_sem.at[r], len(ROUNDS[r]))

    barrier = pltpu.get_barrier_semaphore()
    peers = [{"section": above}, {"section": below}]
    peers += [place(x, z, core) for x, z, core in NEXT]
    for peer in peers:
        pl.semaphore_signal(barrier, inc=1, device_id=peer, device_id_type=MESH)

    low8, low64, low128 = low_of(8), low_of(64), low_of(128)
    for copy in small:
        copy.wait()
    for p in range(2):
        for src, dst, dst_t in ((k_v, keys, keys_t), (v_v, values, values_t)):
            for j in range(2):
                part = src[:, (p + 2 * j) * HD : (p + 2 * j + 1) * HD]
                dst[p, j * SEQ : (j + 1) * SEQ, :] = part
                dst_t[p, :, j * SEQ : (j + 1) * SEQ] = part.T
    for src, dst in ((gain_v, gain_p), (bias_v, bias_p)):
        for h in range(HALF):
            a = jnp.broadcast_to(src[:, h * HD : (h + 1) * HD], (8, HD))
            b = jnp.broadcast_to(src[:, (h + HALF) * HD : (h + HALF + 1) * HD], (8, HD))
            dst[h * 8 : (h + 1) * 8, :] = jnp.where(low8, a, b)
    gain_acc[...] = jnp.zeros_like(gain_acc)
    bias_acc[...] = jnp.zeros_like(bias_acc)
    length = length_ref[0]
    columns = lax.broadcasted_iota(jnp.int32, (8, HD), 1)
    offsets = lax.broadcasted_iota(jnp.int32, (8, HD), 0) & 3

    def forward(b):
        x_copy(b).wait()
        inputs = x_v[pl.ds(b * BLOCK, BLOCK), :].astype(F32)
        inverse = lax.rsqrt(jnp.mean(inputs * inputs, -1, keepdims=True) + 1e-06)
        normed = inputs * inverse
        inverse = jnp.broadcast_to(inverse, (BLOCK, HD))
        gains, biases = gain_p[...], bias_p[...]
        for half in range(2):
            rows = slice(half * 8, half * 8 + 8)
            pair = pack(normed[rows], low8)
            inv = inverse[rows]
            flipped = pltpu.roll(inv, 4, 0)
            pair_inv = (jnp.where(low8, inv, flipped), jnp.where(low8, flipped, inv))
            for j in range(2):
                span = b * PER_BLOCK + half * 2 + j
                norm = pair[j]
                norm_p[span] = norm
                inv_p[span] = pair_inv[j]
                gained = norm * gains
                query = (gained + biases).astype(BF16)
                gained = gained.astype(BF16)
                position = span * ROWS + offsets
                live = tiled(jnp.where(position < length, 1.0, 0.0).astype(F32), 8)
                allowed = tiled(
                    jnp.where((columns <= position) & (columns < length), 1.0, 0.0).astype(F32), 8
                )
                for p in range(2):
                    part = slice(64 * p, 64 * p + 64)
                    query_b[p, span] = query[part]
                    both = dot(jnp.concatenate([query[part], gained[part]], axis=0), keys_t[p])
                    both = pick(both, low128)
                    scores = jnp.where(allowed > 0.5, both[:64] * FACTOR, -1e30)
                    mix_p[span, part, :] = both[64:]
                    weights = jnp.exp(scores - jnp.max(scores, -1, keepdims=True))
                    weights = weights * (1.0 / jnp.sum(weights, -1, keepdims=True)) * live
                    probs_p[span, part, :] = weights * FACTOR
                    wide = spread(weights, low64)
                    high = wide.astype(BF16)
                    probs_b[p, span] = high
                    rest = (wide - high.astype(F32)).astype(BF16)
                    outs = dot(jnp.concatenate([high, rest], axis=0), values[p])
                    base_p[span, part, :] = outs[:64] + outs[64:]

    def take_top(b):
        top_copy(b).wait()
        rows = top_v[pl.ds(b * BLOCK, BLOCK), :].astype(F32)
        for half in range(2):
            pair = pack(rows[half * 8 : half * 8 + 8], low8)
            for j in range(2):
                arrived[b * PER_BLOCK + half * 2 + j] = pair[j].astype(BF16)

    def hop(i):
        return pltpu.make_async_remote_copy(
            src_ref=sent.at[i],
            dst_ref=arrived.at[i],
            send_sem=send_sem.at[i],
            recv_sem=recv_sem.at[i],
            device_id={"section": below},
            device_id_type=MESH,
        )

    def backward(i):
        @pl.when(jnp.logical_not(is_top))
        def _():
            hop(i).wait_recv()

        upstream = arrived[i]
        wide = upstream.astype(F32)
        centre = jnp.sum(wide * base_p[i], -1, keepdims=True)
        queries, kept, totals = [], [], jnp.zeros((8, HD), F32)
        for p in range(2):
            part = slice(64 * p, 64 * p + 64)
            grad_probs = pick(dot(upstream[part], values_t[p]), low64)
            grads = probs_p[i, part, :] * (grad_probs - centre[part])
            totals = totals + jnp.sum((grads * mix_p[i, part, :]).reshape(8, 8, HD), axis=0)
            grads_wide = spread(grads, low64).astype(BF16)
            kept.append(grads_wide)
            queries.append(dot(grads_wide, keys[p]))
        mean = jnp.sum(totals, -1, keepdims=True) * (1.0 / WIDTH)
        mean = jnp.broadcast_to(mean, (8, HD))
        mean = mean + pltpu.roll(mean, 4, 0)
        grad_query = jnp.concatenate(queries, axis=0)
        norm = norm_p[i]
        change = grad_query * gain_p[...] - norm * tiled(mean, HALF)
        sent[i] = (wide + tiled(inv_p[i], HALF) * change).astype(BF16)

        @pl.when((section > 0) & jnp.logical_not(held_back))
        def _():
            hop(i).start()

        @pl.when(held_back & ((2 * i) % 3 > 0))
        def _():
            hop((2 * i + 2) // 3 - 1).start()

        for p in range(2):
            grads_b[p, i] = kept[p]
        gain_acc[...] += grad_query * norm
        bias_acc[...] += grad_query

    behind = sections - 1 - section
    lead = jnp.where(behind == 0, 0, jnp.where(behind == 1, 3, jnp.where(behind == 2, 6, BLOCKS - 1)))

    def prepare(b):
        @pl.when(is_top)
        def _():
            take_top(b)

        forward(b)

    prepare(0)
    pl.semaphore_wait(barrier, len(peers))
    tell(0)

    def turn(t, carry):
        @pl.when(t >= lead)
        def _():
            def step(q, c):
                backward((t - lead) * PER_BLOCK + q)
                return c

            lax.fori_loop(0, PER_BLOCK, step, 0)

        @pl.when(t + 1 < BLOCKS)
        def _():
            prepare(t + 1)

        for r, at in enumerate((2, 4, 6)):

            @pl.when(t == at)
            def _(r=r):
                hear(r)
                tell(r + 1)

        return carry

    lax.fori_loop(0, BLOCKS + lead, turn, 0)

    @pl.when(held_back)
    def _():
        def late(i, carry):
            hop(i).start()
            return carry

        lax.fori_loop(SPANS * 2 // 3, SPANS, late, 0)

    left = lax.broadcasted_iota(jnp.int32, (HALF, HD), 1) < HD // 2
    gain_terms, bias_terms = (acc[...].reshape(HALF, 8, HD) for acc in (gain_acc, bias_acc))
    for j in range(2):
        gain = jnp.sum(gain_terms[:, 4 * j : 4 * j + 4], axis=1)
        bias = jnp.sum(bias_terms[:, 4 * j : 4 * j + 4], axis=1)
        rows = (
            jnp.where(left, gain, pltpu.roll(bias, HD // 2, 1)),
            jnp.where(left, pltpu.roll(gain, HD // 2, 1), bias),
        )
        for h in range(HALF):
            for core in range(DP_CORE):
                share_src[2 * (HALF * j + h) + core] = rows[core][h : h + 1]

    def share_copy(k):
        return pltpu.make_async_remote_copy(
            src_ref=share_src.at[partner(k)],
            dst_ref=share_dst.at[k],
            send_sem=share_sem.at[0],
            recv_sem=share_sem.at[1],
            device_id={"dp": partner(k)},
            device_id_type=MESH,
        )

    hear(len(ROUNDS) - 1)
    for k in range(PARTNERS):
        share_copy(k).start()

    flat = SPANS * 64

    def contract(left, right):
        return lax.dot_general(left, right, (((0,), (0,)), ((), ())), preferred_element_type=F32)

    for p in range(2):
        got = arrived[:, 64 * p : 64 * p + 64, :].reshape(flat, HD)
        value_grad = contract(probs_b[p].reshape(flat, 2 * SEQ), got)
        for j in range(2):
            head = p + 2 * j
            value_out[:, head * HD : (head + 1) * HD] = value_grad[j * SEQ : (j + 1) * SEQ]

    for p in range(2):
        key_grad = contract(grads_b[p].reshape(flat, 2 * SEQ), query_b[p].reshape(flat, HD))
        for j in range(2):
            head = p + 2 * j
            key_out[:, head * HD : (head + 1) * HD] = key_grad[j * SEQ : (j + 1) * SEQ]

    def unpack(b, carry):
        parts = [sent[b * PER_BLOCK + j].astype(F32) for j in range(PER_BLOCK)]
        for h in range(HALF):
            tiles = [part[h * 8 : h * 8 + 8] for part in parts]
            turned = [pltpu.roll(tile, 4, 0) for tile in tiles]
            lower = [jnp.where(low8, tiles[j], turned[j + 1]) for j in (0, 2)]
            upper = [jnp.where(low8, turned[j], tiles[j + 1]) for j in (0, 2)]
            for head, pieces in ((h, lower), (h + HALF, upper)):
                out_ref[pl.ds(b * BLOCK, BLOCK), head * HD : (head + 1) * HD] = jnp.concatenate(
                    pieces, axis=0
                ).astype(BF16)
        return carry

    lax.fori_loop(0, BLOCKS, unpack, 0)

    pltpu.make_async_copy(share_dst, share_dst, share_sem.at[1]).wait()
    share = share_src[me] + jnp.sum(share_dst[...], axis=0)
    gain_out[...] = share[:, : HD // 2]
    bias_out[...] = pltpu.roll(share, HD // 2, 1)[:, : HD // 2]

    def sent_all(i, carry):
        hop(i).wait_send()
        return carry

    @pl.when(section > 0)
    def _():
        lax.fori_loop(0, SPANS, sent_all, 0)

    pltpu.make_async_copy(share_dst, share_dst, share_sem.at[0]).wait()


def write(*refs):
    count = len(refs) // 2
    copies = [
        pltpu.make_async_copy(refs[i], refs[count + i], refs[-1].at[i]) for i in range(count)
    ]
    for copy in copies:
        copy.start()
    for copy in copies:
        copy.wait()


def local(sections, layer_input, keys, values, top_grad, gains, biases, lengths):
    anywhere = pl.BlockSpec(memory_space=pltpu.HBM)
    vmem = pl.BlockSpec(memory_space=pltpu.VMEM)
    kv = KVH * HD
    dma = pltpu.SemaphoreType.DMA
    span = (SPANS, 128, HD)
    outs = pl.pallas_call(
        functools.partial(kernel, sections),
        out_shape=(
            jax.ShapeDtypeStruct((SEQ, WIDTH), BF16),
            jax.ShapeDtypeStruct((SEQ, kv), F32),
            jax.ShapeDtypeStruct((SEQ, kv), F32),
            jax.ShapeDtypeStruct((1, HD // 2), F32),
            jax.ShapeDtypeStruct((1, HD // 2), F32),
        ),
        in_specs=[anywhere] * 6 + [pl.BlockSpec(memory_space=pltpu.SMEM)],
        out_specs=(vmem,) * 5,
        scratch_shapes=[
            pltpu.VMEM((SEQ, WIDTH), BF16),
            pltpu.VMEM((SEQ, WIDTH), BF16),
            pltpu.VMEM((SEQ, kv), BF16),
            pltpu.VMEM((SEQ, kv), BF16),
            pltpu.VMEM((1, WIDTH), F32),
            pltpu.VMEM((1, WIDTH), F32),
            pltpu.VMEM((2, 2 * SEQ, HD), BF16),
            pltpu.VMEM((2, 2 * SEQ, HD), BF16),
            pltpu.VMEM((2, HD, 2 * SEQ), BF16),
            pltpu.VMEM((2, HD, 2 * SEQ), BF16),
            pltpu.VMEM((128, HD), F32),
            pltpu.VMEM((128, HD), F32),
            pltpu.VMEM(span, BF16),
            pltpu.VMEM(span, BF16),
            pltpu.VMEM(span, F32),
            pltpu.VMEM((SPANS, 8, HD), F32),
            pltpu.VMEM(span, F32),
            pltpu.VMEM(span, F32),
            pltpu.VMEM(span, F32),
            pltpu.VMEM((2, SPANS, 64, HD), BF16),
            pltpu.VMEM((2, SPANS, 64, 2 * SEQ), BF16),
            pltpu.VMEM((2, SPANS, 64, 2 * SEQ), BF16),
            pltpu.VMEM((128, HD), F32),
            pltpu.VMEM((128, HD), F32),
            pltpu.VMEM((PARTNERS + 1, 1, HD), F32),
            pltpu.VMEM((PARTNERS, 1, HD), F32),
            dma((4,)),
            dma((BLOCKS,)),
            dma((BLOCKS,)),
            dma((SPANS,)),
            dma((SPANS,)),
            dma((2,)),
            pltpu.SemaphoreType.REGULAR((len(ROUNDS),)),
        ],
        compiler_params=pltpu.CompilerParams(
            collective_id=0, has_side_effects=True, vmem_limit_bytes=40 << 20
        ),
    )(*[pltpu.with_memory_space_constraint(a, pltpu.HBM) for a in (layer_input[0, 0], keys[0, 0], values[0, 0], top_grad[0], gains, biases)], lengths)
    grad_in, key_grad, value_grad, gain_grad, bias_grad = pl.pallas_call(
        write,
        out_shape=tuple(jax.ShapeDtypeStruct(out.shape, out.dtype) for out in outs),
        in_specs=[vmem] * len(outs),
        out_specs=(anywhere,) * len(outs),
        scratch_shapes=[dma((len(outs),))],
        compiler_params=pltpu.CompilerParams(vmem_limit_bytes=4 << 20),
    )(*outs)
    return grad_in[None, None], key_grad[None, None], value_grad[None, None], gain_grad, bias_grad


def solution(mesh):
    return jax.shard_map(
        functools.partial(local, mesh.shape["section"]),
        mesh=mesh,
        in_specs=(
            P("section", "dp", None, None),
            P("section", "dp", None, None),
            P("section", "dp", None, None),
            P("dp", None, None),
            P("section", None),
            P("section", None),
            P("dp"),
        ),
        out_specs=(
            P("section", "dp", None, None),
            P("section", "dp", None, None),
            P("section", "dp", None, None),
            P("section", "dp"),
            P("section", "dp"),
        ),
        check_vma=False,
    )
```

```python
import functools

import jax
import jax.numpy as jnp
from jax import lax
from jax.experimental import pallas as pl
from jax.experimental.pallas import tpu as pltpu
from jax.sharding import PartitionSpec as P

LOGICAL = pl.DeviceIdType.LOGICAL
HD = 128
KVH = 4
SEQ = 128
WIDTH = 4096
ROWS = 4
SPANS = SEQ // ROWS
BLOCK = 16
BLOCKS = SEQ // BLOCK
PER_BLOCK = BLOCK // ROWS
EARLY = 2
GO = 26
HALF = 16
DP_X, DP_Z, DP_CORE = 4, 8, 2
FACTOR = HD ** (-0.5)
F32, BF16 = jnp.float32, jnp.bfloat16
OFFSETS = sorted(
    ((x, z, core) for x in range(DP_X) for z in range(DP_Z) for core in range(DP_CORE)),
    key=lambda at: (-min(at[0], DP_X - at[0]) - min(at[1], DP_Z - at[1]), at),
)
OFFSETS.remove((0, 0, 0))
PARTNERS = len(OFFSETS)
NEXT = ((0, 1, 0), (0, 7, 0), (1, 0, 0), (3, 0, 0), (0, 0, 1))
ROUNDS = (
    ((0, 1, 0), (0, 7, 0), (1, 0, 0), (3, 0, 0)),
    ((0, 2, 0), (0, 6, 0)),
    ((1, 0, 0), (3, 0, 0), (2, 0, 0)),
    ((0, 0, 1),),
)


def dot(a, b):
    return jnp.dot(a, b, preferred_element_type=F32)


def low_of(rows):
    return (lax.broadcasted_iota(jnp.int32, (rows, HD), 0) & 7) < 4


def pick(wide, low):
    return jnp.where(low, wide[:, :HD], wide[:, HD:])


def spread(narrow, low):
    zero = jnp.zeros_like(narrow)
    return jnp.concatenate([jnp.where(low, narrow, zero), jnp.where(low, zero, narrow)], axis=1)


def tiled(eight, times):
    return jnp.concatenate([eight] * times, axis=0)


def pack(eight_rows, low8):
    first, second = [], []
    for h in range(HALF):
        a = eight_rows[:, h * HD : (h + 1) * HD]
        b = eight_rows[:, (h + HALF) * HD : (h + HALF + 1) * HD]
        first.append(jnp.where(low8, a, pltpu.roll(b, 4, 0)))
        second.append(jnp.where(low8, pltpu.roll(a, 4, 0), b))
    return jnp.concatenate(first, axis=0), jnp.concatenate(second, axis=0)


def kernel(
    sections,
    x_hbm, k_hbm, v_hbm, top_hbm, gain_hbm, bias_hbm, length_ref,
    out_ref, key_out, value_out, gain_out, bias_out,
    x_v, top_v, k_v, v_v, gain_v, bias_v,
    keys, values, keys_t, values_t, gain_p, bias_p,
    arrived, sent, norm_p, inv_p, probs_p, mix_p, base_p,
    query_b, probs_b, grads_b, gain_acc, bias_acc,
    share_src, share_dst,
    in_sem, x_sem, top_sem, send_sem, recv_sem, share_sem, round_sem, go_sem,
):
    section = lax.axis_index("section")
    me = lax.axis_index("dp")
    px, pz, pc = me // 16, (me // 2) % 8, me % 2
    above, below = (section + 1) % sections, (section + sections - 1) % sections
    is_top = section == sections - 1
    held_back = is_top & (pc == 1)

    def x_copy(b):
        rows = pl.ds(b * BLOCK, BLOCK)
        return pltpu.make_async_copy(x_hbm.at[rows], x_v.at[rows], x_sem.at[b])

    def top_copy(b):
        rows = pl.ds(b * BLOCK, BLOCK)
        return pltpu.make_async_copy(top_hbm.at[rows], top_v.at[rows], top_sem.at[b])

    small = [
        pltpu.make_async_copy(src, dst, in_sem.at[i])
        for i, (src, dst) in enumerate(
            [(k_hbm, k_v), (v_hbm, v_v), (gain_hbm, gain_v), (bias_hbm, bias_v)]
        )
    ]
    for copy in small:
        copy.start()
    for b in range(BLOCKS):
        x_copy(b).start()

    @pl.when(is_top)
    def _():
        for b in range(BLOCKS):
            top_copy(b).start()

    def partner(k):
        x, z, core = OFFSETS[k]
        return ((px + x) % DP_X) * 16 + ((pz + z) % DP_Z) * 2 + (pc + core) % DP_CORE

    def place(x, z, core):
        dp = ((px + x) % DP_X) * 16 + ((pz + z) % DP_Z) * 2 + (pc + core) % DP_CORE
        return dp * sections + section

    def tell(r):
        for x, z, core in ROUNDS[r]:
            pl.semaphore_signal(
                round_sem.at[r], inc=1, device_id=place(x, z, core), device_id_type=LOGICAL
            )

    def hear(r):
        pl.semaphore_wait(round_sem.at[r], len(ROUNDS[r]))

    barrier = pltpu.get_barrier_semaphore()
    peers = [me * sections + above, me * sections + below]
    peers += [place(x, z, core) for x, z, core in NEXT]
    for peer in peers:
        pl.semaphore_signal(barrier, inc=1, device_id=peer, device_id_type=LOGICAL)

    low8, low64, low128 = low_of(8), low_of(64), low_of(128)
    for copy in small:
        copy.wait()
    for p in range(2):
        for src, dst, dst_t in ((k_v, keys, keys_t), (v_v, values, values_t)):
            for j in range(2):
                part = src[:, (p + 2 * j) * HD : (p + 2 * j + 1) * HD]
                dst[p, j * SEQ : (j + 1) * SEQ, :] = part
                dst_t[p, :, j * SEQ : (j + 1) * SEQ] = part.T
    for src, dst in ((gain_v, gain_p), (bias_v, bias_p)):
        for h in range(HALF):
            a = jnp.broadcast_to(src[:, h * HD : (h + 1) * HD], (8, HD))
            b = jnp.broadcast_to(src[:, (h + HALF) * HD : (h + HALF + 1) * HD], (8, HD))
            dst[h * 8 : (h + 1) * 8, :] = jnp.where(low8, a, b)
    gain_acc[...] = jnp.zeros_like(gain_acc)
    bias_acc[...] = jnp.zeros_like(bias_acc)
    length = length_ref[0]
    columns = lax.broadcasted_iota(jnp.int32, (8, HD), 1)
    offsets = lax.broadcasted_iota(jnp.int32, (8, HD), 0) & 3

    def forward(b):
        x_copy(b).wait()
        inputs = x_v[pl.ds(b * BLOCK, BLOCK), :].astype(F32)
        inverse = lax.rsqrt(jnp.mean(inputs * inputs, -1, keepdims=True) + 1e-06)
        normed = inputs * inverse
        inverse = jnp.broadcast_to(inverse, (BLOCK, HD))
        gains, biases = gain_p[...], bias_p[...]
        items = []
        for half in range(2):
            rows = slice(half * 8, half * 8 + 8)
            pair = pack(normed[rows], low8)
            inv = inverse[rows]
            flipped = pltpu.roll(inv, 4, 0)
            pair_inv = (jnp.where(low8, inv, flipped), jnp.where(low8, flipped, inv))
            for j in range(2):
                span = b * PER_BLOCK + half * 2 + j
                norm = pair[j]
                norm_p[span] = norm
                inv_p[span] = pair_inv[j]
                gained = norm * gains
                query = (gained + biases).astype(BF16)
                gained = gained.astype(BF16)
                for p in range(2):
                    part = slice(64 * p, 64 * p + 64)
                    items.append((span, p, part, query[part], gained[part]))
        boths = [
            pick(dot(jnp.concatenate([query, gained], axis=0), keys_t[p]), low128)
            for _, p, _, query, gained in items
        ]
        results = []
        for (span, p, part, _, _), both in zip(items, boths):
            position = span * ROWS + offsets
            live = tiled(jnp.where(position < length, 1.0, 0.0).astype(F32), 8)
            allowed = tiled(
                jnp.where((columns <= position) & (columns < length), 1.0, 0.0).astype(F32), 8
            )
            scores = jnp.where(allowed > 0.5, both[:64] * FACTOR, -1e30)
            weights = jnp.exp(scores - jnp.max(scores, -1, keepdims=True))
            weights = weights * (1.0 / jnp.sum(weights, -1, keepdims=True)) * live
            wide = spread(weights, low64)
            high = wide.astype(BF16)
            rest = (wide - high.astype(F32)).astype(BF16)
            outs = dot(jnp.concatenate([high, rest], axis=0), values[p])
            results.append((weights, high, outs))
        for (span, p, part, query, _), both, (weights, high, outs) in zip(items, boths, results):
            query_b[p, span] = query
            mix_p[span, part, :] = both[64:]
            probs_p[span, part, :] = weights * FACTOR
            probs_b[p, span] = high
            base_p[span, part, :] = outs[:64] + outs[64:]

    def take_top(b):
        top_copy(b).wait()
        rows = top_v[pl.ds(b * BLOCK, BLOCK), :].astype(F32)
        for half in range(2):
            pair = pack(rows[half * 8 : half * 8 + 8], low8)
            for j in range(2):
                arrived[b * PER_BLOCK + half * 2 + j] = pair[j].astype(BF16)

    def hop(i):
        return pltpu.make_async_remote_copy(
            src_ref=sent.at[i],
            dst_ref=arrived.at[i],
            send_sem=send_sem.at[i],
            recv_sem=recv_sem.at[i],
            device_id=me * sections + below,
            device_id_type=LOGICAL,
        )

    def backward(spans):
        upstreams = [arrived[i] for i in spans]
        wides = [upstream.astype(F32) for upstream in upstreams]
        centres = [jnp.sum(wide * base_p[i], -1, keepdims=True) for i, wide in zip(spans, wides)]
        totals = [jnp.zeros((8, HD), F32) for _ in spans]
        kept, queries = [[] for _ in spans], [[] for _ in spans]
        for p in range(2):
            part = slice(64 * p, 64 * p + 64)
            for n, i in enumerate(spans):
                grad_probs = pick(dot(upstreams[n][part], values_t[p]), low64)
                grads = probs_p[i, part, :] * (grad_probs - centres[n][part])
                mixed = (grads * mix_p[i, part, :]).reshape(8, 8, HD)
                totals[n] = totals[n] + jnp.sum(mixed, axis=0)
                kept[n].append(spread(grads, low64).astype(BF16))
        for p in range(2):
            for n in range(len(spans)):
                queries[n].append(dot(kept[n][p], keys[p]))
        rest = []
        for n, i in enumerate(spans):
            mean = jnp.sum(totals[n], -1, keepdims=True) * (1.0 / WIDTH)
            mean = jnp.broadcast_to(mean, (8, HD))
            mean = mean + pltpu.roll(mean, 4, 0)
            grad_query = jnp.concatenate(queries[n], axis=0)
            norm = norm_p[i]
            change = grad_query * gain_p[...] - norm * tiled(mean, HALF)
            sent[i] = (wides[n] + tiled(inv_p[i], HALF) * change).astype(BF16)
            rest.append((i, kept[n], grad_query, norm))
        return rest

    def finish(rest):
        gains = biases = None
        for i, kept, grad_query, norm in rest:
            for p in range(2):
                grads_b[p, i] = kept[p]
            gained = grad_query * norm
            gains = gained if gains is None else gains + gained
            biases = grad_query if biases is None else biases + grad_query
        gain_acc[...] += gains
        bias_acc[...] += biases

    behind = sections - 1 - section
    lead = jnp.where(behind == 0, 0, jnp.where(behind == 1, 3, jnp.where(behind == 2, 6, BLOCKS - 1)))

    def prepare(b):
        @pl.when(is_top)
        def _():
            take_top(b)

        forward(b)

    prepare(0)
    pl.semaphore_wait(barrier, len(peers))
    tell(0)

    def turn(t, carry):
        @pl.when(is_top)
        def _():
            first = t * PER_BLOCK
            rest = backward([first + q for q in range(PER_BLOCK)])

            @pl.when(pc == 0)
            def _():
                for q in range(PER_BLOCK):
                    hop(first + q).start()

            @pl.when(pc == 1)
            def _():
                for q in range(EARLY):
                    hop(t * EARLY + q).start()

            finish(rest)

        @pl.when((t >= lead) & jnp.logical_not(is_top))
        def _():
            def step(q, c):
                i = (t - lead) * PER_BLOCK + q
                hop(i).wait_recv()
                rest = backward([i])

                @pl.when(section > 0)
                def _():
                    hop(i).start()

                finish(rest)
                return c

            lax.fori_loop(0, PER_BLOCK, step, 0)

        @pl.when(t + 1 < BLOCKS)
        def _():
            prepare(t + 1)

        for r, at in enumerate((2, 4, 6)):

            @pl.when(t == at)
            def _(r=r):
                hear(r)
                tell(r + 1)

        return carry

    lax.fori_loop(0, BLOCKS + lead, turn, 0)

    def sent_some(i, carry):
        hop(i).wait_send()
        return carry

    leader = is_top & (pc == 0)

    @pl.when(leader)
    def _():
        lax.fori_loop(0, GO, sent_some, 0)
        pl.semaphore_signal(go_sem, inc=1, device_id=place(0, 0, 1), device_id_type=LOGICAL)

    @pl.when(held_back)
    def _():
        def late(i, carry):
            hop(i).start()
            return carry

        pl.semaphore_wait(go_sem, 1)
        lax.fori_loop(BLOCKS * EARLY, SPANS, late, 0)

    left = lax.broadcasted_iota(jnp.int32, (HALF, HD), 1) < HD // 2
    gain_terms, bias_terms = (acc[...].reshape(HALF, 8, HD) for acc in (gain_acc, bias_acc))
    for j in range(2):
        gain = jnp.sum(gain_terms[:, 4 * j : 4 * j + 4], axis=1)
        bias = jnp.sum(bias_terms[:, 4 * j : 4 * j + 4], axis=1)
        rows = (
            jnp.where(left, gain, pltpu.roll(bias, HD // 2, 1)),
            jnp.where(left, pltpu.roll(gain, HD // 2, 1), bias),
        )
        for h in range(HALF):
            for core in range(DP_CORE):
                share_src[2 * (HALF * j + h) + core] = rows[core][h : h + 1]

    def share_copy(k):
        return pltpu.make_async_remote_copy(
            src_ref=share_src.at[partner(k)],
            dst_ref=share_dst.at[k],
            send_sem=share_sem.at[0],
            recv_sem=share_sem.at[1],
            device_id=partner(k) * sections + section,
            device_id_type=LOGICAL,
        )

    hear(len(ROUNDS) - 1)
    for k in range(PARTNERS):
        share_copy(k).start()

    flat = SPANS * 64

    def contract(left, right):
        return lax.dot_general(left, right, (((0,), (0,)), ((), ())), preferred_element_type=F32)

    for p in range(2):
        got = arrived[:, 64 * p : 64 * p + 64, :].reshape(flat, HD)
        value_grad = contract(probs_b[p].reshape(flat, 2 * SEQ), got)
        for j in range(2):
            head = p + 2 * j
            value_out[:, head * HD : (head + 1) * HD] = value_grad[j * SEQ : (j + 1) * SEQ]

    for p in range(2):
        key_grad = contract(grads_b[p].reshape(flat, 2 * SEQ), query_b[p].reshape(flat, HD))
        for j in range(2):
            head = p + 2 * j
            key_out[:, head * HD : (head + 1) * HD] = key_grad[j * SEQ : (j + 1) * SEQ]

    def unpack(b, carry):
        parts = [sent[b * PER_BLOCK + j].astype(F32) for j in range(PER_BLOCK)]
        for h in range(HALF):
            tiles = [part[h * 8 : h * 8 + 8] for part in parts]
            turned = [pltpu.roll(tile, 4, 0) for tile in tiles]
            lower = [jnp.where(low8, tiles[j], turned[j + 1]) for j in (0, 2)]
            upper = [jnp.where(low8, turned[j], tiles[j + 1]) for j in (0, 2)]
            for head, pieces in ((h, lower), (h + HALF, upper)):
                out_ref[pl.ds(b * BLOCK, BLOCK), head * HD : (head + 1) * HD] = jnp.concatenate(
                    pieces, axis=0
                ).astype(BF16)
        return carry

    lax.fori_loop(0, BLOCKS, unpack, 0)

    pltpu.make_async_copy(share_dst, share_dst, share_sem.at[1]).wait()
    share = share_src[me] + jnp.sum(share_dst[...], axis=0)
    gain_out[...] = share[:, : HD // 2]
    bias_out[...] = pltpu.roll(share, HD // 2, 1)[:, : HD // 2]

    @pl.when(section > 0)
    def _():
        lax.fori_loop(jnp.where(leader, GO, 0), SPANS, sent_some, 0)

    pltpu.make_async_copy(share_dst, share_dst, share_sem.at[0]).wait()


def write(*refs):
    count = len(refs) // 2
    copies = [
        pltpu.make_async_copy(refs[i], refs[count + i], refs[-1].at[i]) for i in range(count)
    ]
    for copy in copies:
        copy.start()
    for copy in copies:
        copy.wait()


def local(sections, layer_input, keys, values, top_grad, gains, biases, lengths):
    anywhere = pl.BlockSpec(memory_space=pltpu.HBM)
    vmem = pl.BlockSpec(memory_space=pltpu.VMEM)
    kv = KVH * HD
    dma = pltpu.SemaphoreType.DMA
    span = (SPANS, 128, HD)
    outs = pl.pallas_call(
        functools.partial(kernel, sections),
        out_shape=(
            jax.ShapeDtypeStruct((SEQ, WIDTH), BF16),
            jax.ShapeDtypeStruct((SEQ, kv), F32),
            jax.ShapeDtypeStruct((SEQ, kv), F32),
            jax.ShapeDtypeStruct((1, HD // 2), F32),
            jax.ShapeDtypeStruct((1, HD // 2), F32),
        ),
        in_specs=[anywhere] * 6 + [pl.BlockSpec(memory_space=pltpu.SMEM)],
        out_specs=(vmem,) * 5,
        scratch_shapes=[
            pltpu.VMEM((SEQ, WIDTH), BF16),
            pltpu.VMEM((SEQ, WIDTH), BF16),
            pltpu.VMEM((SEQ, kv), BF16),
            pltpu.VMEM((SEQ, kv), BF16),
            pltpu.VMEM((1, WIDTH), F32),
            pltpu.VMEM((1, WIDTH), F32),
            pltpu.VMEM((2, 2 * SEQ, HD), BF16),
            pltpu.VMEM((2, 2 * SEQ, HD), BF16),
            pltpu.VMEM((2, HD, 2 * SEQ), BF16),
            pltpu.VMEM((2, HD, 2 * SEQ), BF16),
            pltpu.VMEM((128, HD), F32),
            pltpu.VMEM((128, HD), F32),
            pltpu.VMEM(span, BF16),
            pltpu.VMEM(span, BF16),
            pltpu.VMEM(span, F32),
            pltpu.VMEM((SPANS, 8, HD), F32),
            pltpu.VMEM(span, F32),
            pltpu.VMEM(span, F32),
            pltpu.VMEM(span, F32),
            pltpu.VMEM((2, SPANS, 64, HD), BF16),
            pltpu.VMEM((2, SPANS, 64, 2 * SEQ), BF16),
            pltpu.VMEM((2, SPANS, 64, 2 * SEQ), BF16),
            pltpu.VMEM((128, HD), F32),
            pltpu.VMEM((128, HD), F32),
            pltpu.VMEM((PARTNERS + 1, 1, HD), F32),
            pltpu.VMEM((PARTNERS, 1, HD), F32),
            dma((4,)),
            dma((BLOCKS,)),
            dma((BLOCKS,)),
            dma((SPANS,)),
            dma((SPANS,)),
            dma((2,)),
            pltpu.SemaphoreType.REGULAR((len(ROUNDS),)),
            pltpu.SemaphoreType.REGULAR,
        ],
        compiler_params=pltpu.CompilerParams(
            collective_id=0, has_side_effects=True, vmem_limit_bytes=40 << 20
        ),
    )(*[pltpu.with_memory_space_constraint(a, pltpu.HBM) for a in (layer_input[0, 0], keys[0, 0], values[0, 0], top_grad[0], gains, biases)], lengths)
    grad_in, key_grad, value_grad, gain_grad, bias_grad = pl.pallas_call(
        write,
        out_shape=tuple(jax.ShapeDtypeStruct(out.shape, out.dtype) for out in outs),
        in_specs=[vmem] * len(outs),
        out_specs=(anywhere,) * len(outs),
        scratch_shapes=[dma((len(outs),))],
        compiler_params=pltpu.CompilerParams(vmem_limit_bytes=4 << 20),
    )(*outs)
    return grad_in[None, None], key_grad[None, None], value_grad[None, None], gain_grad, bias_grad


def solution(mesh):
    return jax.shard_map(
        functools.partial(local, mesh.shape["section"]),
        mesh=mesh,
        in_specs=(
            P("section", "dp", None, None),
            P("section", "dp", None, None),
            P("section", "dp", None, None),
            P("dp", None, None),
            P("section", None),
            P("section", None),
            P("dp"),
        ),
        out_specs=(
            P("section", "dp", None, None),
            P("section", "dp", None, None),
            P("section", "dp", None, None),
            P("section", "dp"),
            P("section", "dp"),
        ),
        check_vma=False,
    )
```

```python
import functools

import jax
import jax.numpy as jnp
from jax import lax
from jax.experimental import pallas as pl
from jax.experimental.pallas import tpu as pltpu
from jax.sharding import PartitionSpec as P

LOGICAL = pl.DeviceIdType.LOGICAL
HD = 128
KVH = 4
SEQ = 128
WIDTH = 4096
ROWS = 4
SPANS = SEQ // ROWS
BLOCK = 16
BLOCKS = SEQ // BLOCK
PER_BLOCK = BLOCK // ROWS
EARLY = 2
GO = 26
PARTS = 4
HALF = 16
DP_X, DP_Z, DP_CORE = 4, 8, 2
FACTOR = HD ** (-0.5)
F32, BF16 = jnp.float32, jnp.bfloat16
OFFSETS = sorted(
    ((x, z, core) for x in range(DP_X) for z in range(DP_Z) for core in range(DP_CORE)),
    key=lambda at: (-min(at[0], DP_X - at[0]) - min(at[1], DP_Z - at[1]), at),
)
OFFSETS.remove((0, 0, 0))
PARTNERS = len(OFFSETS)
NEXT = ((0, 1, 0), (0, 7, 0), (1, 0, 0), (3, 0, 0), (0, 0, 1))
ROUNDS = (
    ((0, 1, 0), (0, 7, 0), (1, 0, 0), (3, 0, 0)),
    ((0, 2, 0), (0, 6, 0)),
    ((1, 0, 0), (3, 0, 0), (2, 0, 0)),
    ((0, 0, 1),),
)


def dot(a, b):
    return jnp.dot(a, b, preferred_element_type=F32)


def low_of(rows):
    return (lax.broadcasted_iota(jnp.int32, (rows, HD), 0) & 7) < 4


def pick(wide, low):
    return jnp.where(low, wide[:, :HD], wide[:, HD:])


def spread(narrow, low):
    zero = jnp.zeros_like(narrow)
    return jnp.concatenate([jnp.where(low, narrow, zero), jnp.where(low, zero, narrow)], axis=1)


def tiled(eight, times):
    return jnp.concatenate([eight] * times, axis=0)


def pack(eight_rows, low8):
    first, second = [], []
    for h in range(HALF):
        a = eight_rows[:, h * HD : (h + 1) * HD]
        b = eight_rows[:, (h + HALF) * HD : (h + HALF + 1) * HD]
        first.append(jnp.where(low8, a, pltpu.roll(b, 4, 0)))
        second.append(jnp.where(low8, pltpu.roll(a, 4, 0), b))
    return jnp.concatenate(first, axis=0), jnp.concatenate(second, axis=0)


def kernel(
    sections,
    x_hbm, k_hbm, v_hbm, top_hbm, gain_hbm, bias_hbm, length_ref,
    out_ref, key_out, value_out, gain_out, bias_out,
    x_v, top_v, k_v, v_v, gain_v, bias_v,
    keys, values, keys_t, values_t, gain_p, bias_p,
    arrived, sent, norm_p, inv_p, probs_p, mix_p, base_p,
    query_b, probs_b, grads_b, gain_acc, bias_acc,
    share_src, share_dst,
    in_sem, x_sem, top_sem, send_sem, recv_sem, share_sem, round_sem, go_sem,
):
    section = lax.axis_index("section")
    me = lax.axis_index("dp")
    px, pz, pc = me // 16, (me // 2) % 8, me % 2
    above, below = (section + 1) % sections, (section + sections - 1) % sections
    is_top = section == sections - 1
    held_back = is_top & (pc == 1)

    def x_copy(b):
        rows = pl.ds(b * BLOCK, BLOCK)
        return pltpu.make_async_copy(x_hbm.at[rows], x_v.at[rows], x_sem.at[b])

    def top_copy(b):
        rows = pl.ds(b * BLOCK, BLOCK)
        return pltpu.make_async_copy(top_hbm.at[rows], top_v.at[rows], top_sem.at[b])

    small = [
        pltpu.make_async_copy(src, dst, in_sem.at[i])
        for i, (src, dst) in enumerate(
            [(k_hbm, k_v), (v_hbm, v_v), (gain_hbm, gain_v), (bias_hbm, bias_v)]
        )
    ]
    for copy in small:
        copy.start()
    for b in range(BLOCKS):
        x_copy(b).start()

    @pl.when(is_top)
    def _():
        for b in range(BLOCKS):
            top_copy(b).start()

    def partner(k):
        x, z, core = OFFSETS[k]
        return ((px + x) % DP_X) * 16 + ((pz + z) % DP_Z) * 2 + (pc + core) % DP_CORE

    def place(x, z, core):
        dp = ((px + x) % DP_X) * 16 + ((pz + z) % DP_Z) * 2 + (pc + core) % DP_CORE
        return dp * sections + section

    def tell(r):
        for x, z, core in ROUNDS[r]:
            pl.semaphore_signal(
                round_sem.at[r], inc=1, device_id=place(x, z, core), device_id_type=LOGICAL
            )

    def hear(r):
        pl.semaphore_wait(round_sem.at[r], len(ROUNDS[r]))

    barrier = pltpu.get_barrier_semaphore()
    peers = [me * sections + above, me * sections + below]
    peers += [place(x, z, core) for x, z, core in NEXT]
    for peer in peers:
        pl.semaphore_signal(barrier, inc=1, device_id=peer, device_id_type=LOGICAL)

    low8, low64, low128 = low_of(8), low_of(64), low_of(128)
    for copy in small:
        copy.wait()
    for p in range(2):
        for src, dst, dst_t in ((k_v, keys, keys_t), (v_v, values, values_t)):
            for j in range(2):
                part = src[:, (p + 2 * j) * HD : (p + 2 * j + 1) * HD]
                dst[p, j * SEQ : (j + 1) * SEQ, :] = part
                dst_t[p, :, j * SEQ : (j + 1) * SEQ] = part.T
    for src, dst in ((gain_v, gain_p), (bias_v, bias_p)):
        for h in range(HALF):
            a = jnp.broadcast_to(src[:, h * HD : (h + 1) * HD], (8, HD))
            b = jnp.broadcast_to(src[:, (h + HALF) * HD : (h + HALF + 1) * HD], (8, HD))
            dst[h * 8 : (h + 1) * 8, :] = jnp.where(low8, a, b)
    gain_acc[...] = jnp.zeros_like(gain_acc)
    bias_acc[...] = jnp.zeros_like(bias_acc)
    length = length_ref[0]
    columns = lax.broadcasted_iota(jnp.int32, (8, HD), 1)
    offsets = lax.broadcasted_iota(jnp.int32, (8, HD), 0) & 3

    def forward(b):
        x_copy(b).wait()
        inputs = x_v[pl.ds(b * BLOCK, BLOCK), :].astype(F32)
        inverse = lax.rsqrt(jnp.mean(inputs * inputs, -1, keepdims=True) + 1e-06)
        normed = inputs * inverse
        inverse = jnp.broadcast_to(inverse, (BLOCK, HD))
        gains, biases = gain_p[...], bias_p[...]
        items = []
        for half in range(2):
            rows = slice(half * 8, half * 8 + 8)
            pair = pack(normed[rows], low8)
            inv = inverse[rows]
            flipped = pltpu.roll(inv, 4, 0)
            pair_inv = (jnp.where(low8, inv, flipped), jnp.where(low8, flipped, inv))
            for j in range(2):
                span = b * PER_BLOCK + half * 2 + j
                norm = pair[j]
                norm_p[span] = norm
                inv_p[span] = pair_inv[j]
                gained = norm * gains
                query = (gained + biases).astype(BF16)
                gained = gained.astype(BF16)
                for p in range(2):
                    part = slice(64 * p, 64 * p + 64)
                    items.append((span, p, part, query[part], gained[part]))
        boths = [
            pick(dot(jnp.concatenate([query, gained], axis=0), keys_t[p]), low128)
            for _, p, _, query, gained in items
        ]
        results = []
        for (span, p, part, _, _), both in zip(items, boths):
            position = span * ROWS + offsets
            live = tiled(jnp.where(position < length, 1.0, 0.0).astype(F32), 8)
            allowed = tiled(
                jnp.where((columns <= position) & (columns < length), 1.0, 0.0).astype(F32), 8
            )
            scores = jnp.where(allowed > 0.5, both[:64] * FACTOR, -1e30)
            weights = jnp.exp(scores - jnp.max(scores, -1, keepdims=True))
            weights = weights * (1.0 / jnp.sum(weights, -1, keepdims=True)) * live
            wide = spread(weights, low64)
            high = wide.astype(BF16)
            rest = (wide - high.astype(F32)).astype(BF16)
            outs = dot(jnp.concatenate([high, rest], axis=0), values[p])
            results.append((weights, high, outs))
        for (span, p, part, query, _), both, (weights, high, outs) in zip(items, boths, results):
            query_b[p, span] = query
            mix_p[span, part, :] = both[64:]
            probs_p[span, part, :] = weights * FACTOR
            probs_b[p, span] = high
            base_p[span, part, :] = outs[:64] + outs[64:]

    def take_top(b):
        top_copy(b).wait()
        rows = top_v[pl.ds(b * BLOCK, BLOCK), :].astype(F32)
        for half in range(2):
            pair = pack(rows[half * 8 : half * 8 + 8], low8)
            for j in range(2):
                arrived[b * PER_BLOCK + half * 2 + j] = pair[j].astype(BF16)

    def hop(i):
        return pltpu.make_async_remote_copy(
            src_ref=sent.at[i],
            dst_ref=arrived.at[i],
            send_sem=send_sem.at[i],
            recv_sem=recv_sem.at[i],
            device_id=me * sections + below,
            device_id_type=LOGICAL,
        )

    def backward(spans):
        upstreams = [arrived[i] for i in spans]
        wides = [upstream.astype(F32) for upstream in upstreams]
        centres = [jnp.sum(wide * base_p[i], -1, keepdims=True) for i, wide in zip(spans, wides)]
        totals = [jnp.zeros((8, HD), F32) for _ in spans]
        kept, queries = [[] for _ in spans], [[] for _ in spans]
        for p in range(2):
            part = slice(64 * p, 64 * p + 64)
            for n, i in enumerate(spans):
                grad_probs = pick(dot(upstreams[n][part], values_t[p]), low64)
                grads = probs_p[i, part, :] * (grad_probs - centres[n][part])
                mixed = (grads * mix_p[i, part, :]).reshape(8, 8, HD)
                totals[n] = totals[n] + jnp.sum(mixed, axis=0)
                kept[n].append(spread(grads, low64).astype(BF16))
        for p in range(2):
            for n in range(len(spans)):
                queries[n].append(dot(kept[n][p], keys[p]))
        rest = []
        for n, i in enumerate(spans):
            mean = jnp.sum(totals[n], -1, keepdims=True) * (1.0 / WIDTH)
            mean = jnp.broadcast_to(mean, (8, HD))
            mean = mean + pltpu.roll(mean, 4, 0)
            grad_query = jnp.concatenate(queries[n], axis=0)
            norm = norm_p[i]
            change = grad_query * gain_p[...] - norm * tiled(mean, HALF)
            sent[i] = (wides[n] + tiled(inv_p[i], HALF) * change).astype(BF16)
            rest.append((i, kept[n], grad_query, norm))
        return rest

    def finish(rest):
        gains = biases = None
        for i, kept, grad_query, norm in rest:
            for p in range(2):
                grads_b[p, i] = kept[p]
            gained = grad_query * norm
            gains = gained if gains is None else gains + gained
            biases = grad_query if biases is None else biases + grad_query
        gain_acc[...] += gains
        bias_acc[...] += biases

    behind = sections - 1 - section
    lead = jnp.where(behind == 0, 0, jnp.where(behind == 1, 3, jnp.where(behind == 2, 6, BLOCKS - 1)))

    def prepare(b):
        @pl.when(is_top)
        def _():
            take_top(b)

        forward(b)

    prepare(0)
    pl.semaphore_wait(barrier, len(peers))
    tell(0)

    def turn(t, carry):
        @pl.when(is_top)
        def _():
            first = t * PER_BLOCK
            rest = backward([first + q for q in range(PER_BLOCK)])

            @pl.when(pc == 0)
            def _():
                for q in range(PER_BLOCK):
                    hop(first + q).start()

            @pl.when(pc == 1)
            def _():
                for q in range(EARLY):
                    hop(t * EARLY + q).start()

            finish(rest)

        @pl.when((t >= lead) & jnp.logical_not(is_top))
        def _():
            def step(q, c):
                i = (t - lead) * PER_BLOCK + q
                hop(i).wait_recv()
                rest = backward([i])

                @pl.when(section > 0)
                def _():
                    hop(i).start()

                finish(rest)
                return c

            lax.fori_loop(0, PER_BLOCK, step, 0)

        @pl.when(t + 1 < BLOCKS)
        def _():
            prepare(t + 1)

        for r, at in enumerate((2, 4, 6)):

            @pl.when(t == at)
            def _(r=r):
                hear(r)
                tell(r + 1)

        return carry

    lax.fori_loop(0, BLOCKS + lead, turn, 0)

    def sent_some(i, carry):
        hop(i).wait_send()
        return carry

    leader = is_top & (pc == 0)

    @pl.when(leader)
    def _():
        lax.fori_loop(0, GO, sent_some, 0)
        pl.semaphore_signal(go_sem, inc=1, device_id=place(0, 0, 1), device_id_type=LOGICAL)

    @pl.when(held_back)
    def _():
        def late(i, carry):
            hop(i).start()
            return carry

        pl.semaphore_wait(go_sem, 1)
        lax.fori_loop(BLOCKS * EARLY, SPANS, late, 0)

    left = lax.broadcasted_iota(jnp.int32, (HALF, HD), 1) < HD // 2
    gain_terms, bias_terms = (acc[...].reshape(HALF, 8, HD) for acc in (gain_acc, bias_acc))
    for j in range(2):
        gain = jnp.sum(gain_terms[:, 4 * j : 4 * j + 4], axis=1)
        bias = jnp.sum(bias_terms[:, 4 * j : 4 * j + 4], axis=1)
        rows = (
            jnp.where(left, gain, pltpu.roll(bias, HD // 2, 1)),
            jnp.where(left, pltpu.roll(gain, HD // 2, 1), bias),
        )
        for h in range(HALF):
            for core in range(DP_CORE):
                share_src[2 * (HALF * j + h) + core] = rows[core][h : h + 1]

    def share_copy(k):
        return pltpu.make_async_remote_copy(
            src_ref=share_src.at[partner(k)],
            dst_ref=share_dst.at[k],
            send_sem=share_sem.at[0],
            recv_sem=share_sem.at[1],
            device_id=partner(k) * sections + section,
            device_id_type=LOGICAL,
        )

    hear(len(ROUNDS) - 1)
    for k in range(PARTNERS):
        share_copy(k).start()

    flat = SPANS * 64

    def contract(left, right):
        return lax.dot_general(left, right, (((0,), (0,)), ((), ())), preferred_element_type=F32)

    for p in range(2):
        got = arrived[:, 64 * p : 64 * p + 64, :].reshape(flat, HD)
        value_grad = contract(probs_b[p].reshape(flat, 2 * SEQ), got)
        for j in range(2):
            head = p + 2 * j
            value_out[:, head * HD : (head + 1) * HD] = value_grad[j * SEQ : (j + 1) * SEQ]

    for p in range(2):
        key_grad = contract(grads_b[p].reshape(flat, 2 * SEQ), query_b[p].reshape(flat, HD))
        for j in range(2):
            head = p + 2 * j
            key_out[:, head * HD : (head + 1) * HD] = key_grad[j * SEQ : (j + 1) * SEQ]

    def unpack(b, carry):
        parts = [sent[b * PER_BLOCK + j].astype(F32) for j in range(PER_BLOCK)]
        for h in range(HALF):
            tiles = [part[h * 8 : h * 8 + 8] for part in parts]
            turned = [pltpu.roll(tile, 4, 0) for tile in tiles]
            lower = [jnp.where(low8, tiles[j], turned[j + 1]) for j in (0, 2)]
            upper = [jnp.where(low8, turned[j], tiles[j + 1]) for j in (0, 2)]
            for head, pieces in ((h, lower), (h + HALF, upper)):
                out_ref[pl.ds(b * BLOCK, BLOCK), head * HD : (head + 1) * HD] = jnp.concatenate(
                    pieces, axis=0
                ).astype(BF16)
        return carry

    lax.fori_loop(0, BLOCKS, unpack, 0)

    pltpu.make_async_copy(share_dst, share_dst, share_sem.at[1]).wait()
    share = share_src[me] + jnp.sum(share_dst[...], axis=0)
    gain_out[...] = share[:, : HD // 2]
    bias_out[...] = pltpu.roll(share, HD // 2, 1)[:, : HD // 2]

    @pl.when(section > 0)
    def _():
        lax.fori_loop(jnp.where(leader, GO, 0), SPANS, sent_some, 0)

    pltpu.make_async_copy(share_dst, share_dst, share_sem.at[0]).wait()


def write(*refs):
    count = len(refs) // 2
    pairs = [(refs[i], refs[count + i]) for i in range(1, count)]
    for part in range(PARTS):
        rows = pl.ds(part * (SEQ // PARTS), SEQ // PARTS)
        pairs.append((refs[0].at[rows], refs[count].at[rows]))
    copies = [
        pltpu.make_async_copy(src, dst, refs[-1].at[i]) for i, (src, dst) in enumerate(pairs)
    ]
    for copy in copies:
        copy.start()
    for copy in copies:
        copy.wait()


def local(sections, layer_input, keys, values, top_grad, gains, biases, lengths):
    anywhere = pl.BlockSpec(memory_space=pltpu.HBM)
    vmem = pl.BlockSpec(memory_space=pltpu.VMEM)
    kv = KVH * HD
    dma = pltpu.SemaphoreType.DMA
    span = (SPANS, 128, HD)
    outs = pl.pallas_call(
        functools.partial(kernel, sections),
        out_shape=(
            jax.ShapeDtypeStruct((SEQ, WIDTH), BF16),
            jax.ShapeDtypeStruct((SEQ, kv), F32),
            jax.ShapeDtypeStruct((SEQ, kv), F32),
            jax.ShapeDtypeStruct((1, HD // 2), F32),
            jax.ShapeDtypeStruct((1, HD // 2), F32),
        ),
        in_specs=[anywhere] * 6 + [pl.BlockSpec(memory_space=pltpu.SMEM)],
        out_specs=(vmem,) * 5,
        scratch_shapes=[
            pltpu.VMEM((SEQ, WIDTH), BF16),
            pltpu.VMEM((SEQ, WIDTH), BF16),
            pltpu.VMEM((SEQ, kv), BF16),
            pltpu.VMEM((SEQ, kv), BF16),
            pltpu.VMEM((1, WIDTH), F32),
            pltpu.VMEM((1, WIDTH), F32),
            pltpu.VMEM((2, 2 * SEQ, HD), BF16),
            pltpu.VMEM((2, 2 * SEQ, HD), BF16),
            pltpu.VMEM((2, HD, 2 * SEQ), BF16),
            pltpu.VMEM((2, HD, 2 * SEQ), BF16),
            pltpu.VMEM((128, HD), F32),
            pltpu.VMEM((128, HD), F32),
            pltpu.VMEM(span, BF16),
            pltpu.VMEM(span, BF16),
            pltpu.VMEM(span, F32),
            pltpu.VMEM((SPANS, 8, HD), F32),
            pltpu.VMEM(span, F32),
            pltpu.VMEM(span, F32),
            pltpu.VMEM(span, F32),
            pltpu.VMEM((2, SPANS, 64, HD), BF16),
            pltpu.VMEM((2, SPANS, 64, 2 * SEQ), BF16),
            pltpu.VMEM((2, SPANS, 64, 2 * SEQ), BF16),
            pltpu.VMEM((128, HD), F32),
            pltpu.VMEM((128, HD), F32),
            pltpu.VMEM((PARTNERS + 1, 1, HD), F32),
            pltpu.VMEM((PARTNERS, 1, HD), F32),
            dma((4,)),
            dma((BLOCKS,)),
            dma((BLOCKS,)),
            dma((SPANS,)),
            dma((SPANS,)),
            dma((2,)),
            pltpu.SemaphoreType.REGULAR((len(ROUNDS),)),
            pltpu.SemaphoreType.REGULAR,
        ],
        compiler_params=pltpu.CompilerParams(
            collective_id=0, has_side_effects=True, vmem_limit_bytes=40 << 20
        ),
    )(*[pltpu.with_memory_space_constraint(a, pltpu.HBM) for a in (layer_input[0, 0], keys[0, 0], values[0, 0], top_grad[0], gains, biases)], lengths)
    grad_in, key_grad, value_grad, gain_grad, bias_grad = pl.pallas_call(
        write,
        out_shape=tuple(jax.ShapeDtypeStruct(out.shape, out.dtype) for out in outs),
        in_specs=[vmem] * len(outs),
        out_specs=(anywhere,) * len(outs),
        scratch_shapes=[dma((len(outs) - 1 + PARTS,))],
        compiler_params=pltpu.CompilerParams(vmem_limit_bytes=4 << 20),
    )(*outs)
    return grad_in[None, None], key_grad[None, None], value_grad[None, None], gain_grad, bias_grad


def solution(mesh):
    return jax.shard_map(
        functools.partial(local, mesh.shape["section"]),
        mesh=mesh,
        in_specs=(
            P("section", "dp", None, None),
            P("section", "dp", None, None),
            P("section", "dp", None, None),
            P("dp", None, None),
            P("section", None),
            P("section", None),
            P("dp"),
        ),
        out_specs=(
            P("section", "dp", None, None),
            P("section", "dp", None, None),
            P("section", "dp", None, None),
            P("section", "dp"),
            P("section", "dp"),
        ),
        check_vma=False,
    )
```
